128 devices in a mesh: sector: 8 (over z, core), table: 16 (over y, x).
Axes of the slice: x: 4, y: 4, z: 4, core: 2. Of those that a mesh axis runs over, the one named last changes fastest.
Arguments:
- wave_blocks: bfloat16 [64, 256, 256], P('sector', 'table'), may hold values from -6 to 6
- recoupling: bfloat16 [256, 256, 256], P('table'), may hold values from -0.375 to 0.375
- right_blocks: bfloat16 [64, 256, 256], P('sector'), may hold values from -0.02734375 to 0.02734375
- sector_sizes: int32 [64], P('sector'), may hold values from 128 to 256
- channel_env: int32 [64, 2], P('sector'), may hold values from 0 to 7
- fetch_list: int32 [8, 8, 3], P('sector'), may hold values from 0 to 7
- term_pick: int32 [24576], P(('sector', 'table')), may hold values from 0 to 23
- term_table: int32 [24576], P(('sector', 'table')), may hold values from 0 to 15
- term_slot: int32 [24576], P(('sector', 'table')), may hold values from 0 to 15
- term_live: int32 [24576], P(('sector', 'table')), may hold values from 0 to 1, as said below
Outputs:
- sigma_blocks: float32 [64, 256, 256], P('sector', 'table')
The draws below stay inside these ranges and needn't reach their ends.
Inputs may be any that keep to these rules, and one draw needn't show every extreme that they name: `term_live`: in each aligned block of 192 terms (one device's) the live terms come first; some block is all live.
All inputs are finite; a program needn't handle non-finite values.
Results may differ from the reference program's by a relative error of at most 0.0003.
Values may be sent and summed in bfloat16 or wider, within the bound.
No kernel may reach another device: no remote copies, remote signals or barrier semaphores. Data moves between devices by JAX's collectives and lax.ppermute only.
A program may use at most 128 MiB of HBM per device.

```python
import jax
import jax.numpy as jnp
from jax import lax

BLOCK = 256
SEC_DEV = 8
CHANNELS = 2
ENV_DEV = 8
TAB_DEV = 16
LISTED = 3
TERM_DEV = 192
GROUPS = 8
SHARDS = 16
SECTORS = 64
TABLES = 256
ENVS = 64
TERMS_GROUP = 3072
TERMS = 24576
PICKS = 24


def draw_term_live(key, part):
    key = jax.random.fold_in(key, 7)
    first_key, second_key = jax.random.split(key)
    blocks_all = TERMS // TERM_DEV
    divisor = jax.random.randint(first_key, (blocks_all,), 1, 5)
    counts = TERM_DEV // divisor
    fullest = jax.random.randint(second_key, (), 0, blocks_all)
    counts = jnp.where(jnp.arange(blocks_all) == fullest, TERM_DEV, counts)
    position = jnp.arange(TERMS) % TERM_DEV
    return (position < jnp.repeat(counts, TERM_DEV)).astype(jnp.int32)


def set_ends(array, key, least, high):
    extent = array.shape
    place = [jax.random.randint(jax.random.fold_in(key, axis), (), 0, extent[axis]) for axis in range(len(extent))]
    array = array.at[tuple(place)].set(least)
    longest = extent.index(max(extent))
    place[longest] = (place[longest] + 1) % extent[longest]
    return array.at[tuple(place)].set(high)


def block_levels(own_key, extent, shards, smallest, high):
    def one(dim, blocks):
        steps = jax.random.uniform(jax.random.fold_in(jax.random.fold_in(own_key, 6), dim), (blocks,), jnp.float32, smallest / len(shards), high / len(shards))
        return jnp.repeat(jnp.exp(steps), extent[dim] // blocks).reshape((-1,) + (1,) * (len(extent) - dim - 1))

    level = one(*shards[0])
    for cut in shards[1:]:
        level = level * one(*cut)
    return level


def bell_draw(rng, dims, scale, reach, cuts=(), held_as=jnp.bfloat16):
    values = jax.random.normal(rng, dims, jnp.float32) * scale
    if len(cuts) > 0:
        values = block_levels(rng, dims, cuts, -0.22, 0.18) * values
    return jnp.clip(values, min=-reach, max=reach).astype(held_as)


def setup_inputs(seed: int = 0) -> dict:
    arg_keys = jax.random.split(jax.random.key(seed), 11)
    wave_blocks = bell_draw(arg_keys[0], (SECTORS, BLOCK, BLOCK), 1.0, 6.0, ((0, 8), (1, 16)))
    recoupling = bell_draw(arg_keys[1], (TABLES, BLOCK, BLOCK), BLOCK ** -0.5, 0.375, ((0, 16),))
    right_blocks = bell_draw(arg_keys[2], (ENVS, BLOCK, BLOCK), (BLOCK * TERMS_GROUP // (2 * SEC_DEV)) ** -0.5, 0.02734375, ((0, 8),))
    sector_sizes = set_ends(jax.random.randint(arg_keys[3], (SECTORS,), BLOCK // 2, BLOCK + 1), jax.random.fold_in(arg_keys[3], 1), BLOCK // 2, BLOCK).astype(jnp.int32)
    channel_env = set_ends(jax.random.randint(arg_keys[4], (SECTORS, CHANNELS), 0, ENV_DEV), jax.random.fold_in(arg_keys[4], 1), 0, ENV_DEV - 1).astype(jnp.int32)
    fetch_list = set_ends(jax.random.randint(arg_keys[5], (GROUPS, GROUPS, LISTED), 0, SEC_DEV), jax.random.fold_in(arg_keys[5], 1), 0, SEC_DEV - 1).astype(jnp.int32)
    term_pick = set_ends(jax.random.randint(arg_keys[6], (TERMS,), 0, PICKS), jax.random.fold_in(arg_keys[6], 1), 0, PICKS - 1).astype(jnp.int32)
    term_table = set_ends(jax.random.randint(arg_keys[7], (TERMS,), 0, TAB_DEV), jax.random.fold_in(arg_keys[7], 1), 0, TAB_DEV - 1).astype(jnp.int32)
    term_slot = set_ends(jax.random.randint(arg_keys[8], (TERMS,), 0, SEC_DEV * CHANNELS), jax.random.fold_in(arg_keys[8], 1), 0, (SEC_DEV * CHANNELS) - 1).astype(jnp.int32)
    term_live = draw_term_live(jax.random.fold_in(arg_keys[10], 71), 0)
    return dict(wave_blocks=wave_blocks, recoupling=recoupling, right_blocks=right_blocks, sector_sizes=sector_sizes, channel_env=channel_env, fetch_list=fetch_list, term_pick=term_pick, term_table=term_table, term_slot=term_slot, term_live=term_live)


def reference(wave_blocks, recoupling, right_blocks, sector_sizes, channel_env, fetch_list, term_pick, term_table, term_slot, term_live):
    slots_group = SEC_DEV * CHANNELS
    order_ids = jnp.arange(TERMS, dtype=jnp.int32)
    block_ids = order_ids // TERM_DEV
    group_ids = block_ids // SHARDS
    shard_ids = block_ids % SHARDS
    listed_group = term_pick // LISTED
    listed_column = term_pick % LISTED
    sources = listed_group * SEC_DEV + fetch_list[group_ids, listed_group, listed_column]
    table_ids = shard_ids * TAB_DEV + term_table
    slot_ids = group_ids * slots_group + term_slot
    weights = term_live.astype(jnp.float32)

    def accumulate(totals, pieces):
        src_ids, tab_ids, out_ids, live_weights = pieces
        left_side = recoupling[tab_ids].astype(jnp.float32)
        right_side = wave_blocks[src_ids].astype(jnp.float32)
        product = jnp.einsum("tij,tjk->tik", left_side, right_side, precision=lax.Precision.HIGHEST)
        return totals.at[out_ids].add(product * live_weights[:, None, None]), None

    pieces = (sources.reshape(-1, 32), table_ids.reshape(-1, 32), slot_ids.reshape(-1, 32), weights.reshape(-1, 32))
    channel, _ = lax.scan(accumulate, jnp.zeros((SECTORS * CHANNELS, BLOCK, BLOCK), jnp.float32), pieces)
    owners = (jnp.arange(SECTORS, dtype=jnp.int32) // SEC_DEV)[:, None] * ENV_DEV + channel_env
    env_blocks = right_blocks[owners].astype(jnp.float32)
    result = jnp.einsum("opij,opjk->oik", channel.reshape(SECTORS, CHANNELS, BLOCK, BLOCK), env_blocks, precision=lax.Precision.HIGHEST)
    line_ids = jnp.arange(BLOCK, dtype=jnp.int32)
    limits = sector_sizes[:, None, None]
    keep = (line_ids[None, :, None] < limits) & (line_ids[None, None, :] < limits)
    return jnp.where(keep, result, jnp.float32(0.0))
```

```python
import functools

import jax
import jax.numpy as jnp
from jax import lax
from jax.experimental import pallas as pl
from jax.experimental.pallas import tpu as pltpu
from jax.sharding import PartitionSpec as P

BF = jnp.bfloat16
F32 = jnp.float32
SIDE = 4
TABS = 16
ROWS = 16
HALF = 64
WIDTH = 256
SLOTS = 16
PICKS = 24
PAIRS = SLOTS * PICKS
SHARE = ROWS * 128
SENT = SHARE + PAIRS
DEPTH = PICKS * HALF
MIB = 1 << 20


def swap_halves(value):
    return pltpu.roll(value, 64, 1)


def pack_kernel(meta, t0_ref, t1_ref, terms_ref, out_ref, rows0, rows1, count):
    low = lax.broadcasted_iota(jnp.int32, (TABS, 128), 1) < 64

    @pl.when(pl.program_id(0) == 0)
    def _():
        pair = terms_ref[0:1, :]
        tab = terms_ref[1:2, :]
        live = terms_ref[2:3, :]
        terms = terms_ref.shape[1]
        tab_hot = (lax.broadcasted_iota(jnp.int32, (TABS, terms), 0) == tab) & (live > 0)
        pair_hot = lax.broadcasted_iota(jnp.int32, (PAIRS, terms), 0) == pair
        counts = lax.dot_general(
            tab_hot.astype(F32).astype(BF),
            pair_hot.astype(F32).astype(BF),
            (((1,), (1,)), ((), ())),
            preferred_element_type=F32,
        )
        count[...] = counts.astype(BF)

    for k in range(2):
        rows0[k] = t0_ref[:, 0, :, k * 128 : k * 128 + 128].reshape(TABS * ROWS, 128).astype(F32)
        rows1[k] = t1_ref[:, 0, :, k * 128 : k * 128 + 128].reshape(TABS * ROWS, 128).astype(F32)
    for y in range(SIDE):
        out_ref[y, 0, :, SHARE:SENT] = count[...]
    for q in range(ROWS):
        lanes = slice(q * 128, q * 128 + 128)
        for k in range(2):
            a = rows0[k, pl.ds(q, TABS, stride=ROWS), :]
            b = rows1[k, pl.ds(q, TABS, stride=ROWS), :]
            out_ref[2 * k, 0, :, lanes] = jnp.where(low, a, swap_halves(b)).astype(BF)
            out_ref[2 * k + 1, 0, :, lanes] = jnp.where(low, swap_halves(a), b).astype(BF)


def pack(core, recoupling, terms):
    blocks = recoupling.reshape(TABS, SIDE, HALF, WIDTH)
    out = pl.pallas_call(
        pack_kernel,
        grid_spec=pltpu.PrefetchScalarGridSpec(
            num_scalar_prefetch=1,
            grid=(SIDE,),
            in_specs=[
                pl.BlockSpec((TABS, 1, ROWS, WIDTH), lambda x, m: (0, m[0], x, 0)),
                pl.BlockSpec((TABS, 1, ROWS, WIDTH), lambda x, m: (0, m[0] + 2, x, 0)),
                pl.BlockSpec(terms.shape, lambda x, m: (0, 0)),
            ],
            out_specs=pl.BlockSpec((SIDE, 1, TABS, SENT), lambda x, m: (0, x, 0, 0)),
            scratch_shapes=[
                pltpu.VMEM((2, TABS * ROWS, 128), F32),
                pltpu.VMEM((2, TABS * ROWS, 128), F32),
                pltpu.VMEM((TABS, PAIRS), BF),
            ],
        ),
        out_shape=jax.ShapeDtypeStruct((SIDE, SIDE, TABS, SENT), BF),
        compiler_params=pltpu.CompilerParams(vmem_limit_bytes=24 * MIB),
        name="pack",
    )(core, blocks, blocks, terms)
    return out.reshape(SIDE * SIDE, TABS, SENT)


def select_kernel(meta, w0, w1, w2, w3, out_ref):
    z = meta[0]
    core = meta[1]
    for p in range(PICKS):
        group = p // 3
        piece = meta[2 + p]
        step = lax.rem(z - group // 2 + SIDE, SIDE)
        other = jnp.where(core == group % 2, 0, 1)
        for d, ref in enumerate((w0, w1, w2, w3)):

            @pl.when(step == d)
            def _(ref=ref, p=p, other=other, piece=piece):
                out_ref[p] = ref[other * 8 + piece]


def select(meta, pieces):
    return pl.pallas_call(
        select_kernel,
        in_specs=[pl.BlockSpec(memory_space=pltpu.SMEM)] + [pl.BlockSpec(memory_space=pltpu.VMEM)] * 4,
        out_specs=pl.BlockSpec(memory_space=pltpu.VMEM),
        out_shape=jax.ShapeDtypeStruct((PICKS, ROWS, WIDTH), BF),
        compiler_params=pltpu.CompilerParams(vmem_limit_bytes=8 * MIB),
        name="select",
    )(meta, *pieces)


def weigh_kernel(c_ref, t_ref, hi_ref, lo_ref, sums):
    counts = c_ref[...]
    for n in range(ROWS // 2):
        part = lax.dot_general(
            counts, t_ref[:, n * 256 : n * 256 + 256], (((0,), (0,)), ((), ())), preferred_element_type=F32
        )
        sums[2 * n * PAIRS : (2 * n + 1) * PAIRS, :] = part[:, :128]
        sums[(2 * n + 1) * PAIRS : (2 * n + 2) * PAIRS, :] = part[:, 128:]
    low = lax.broadcasted_iota(jnp.int32, (ROWS, 128), 1) < 64

    def one(s, carry):
        for k in range(PICKS // 2):
            row = s * PICKS + 2 * k
            a = sums[pl.ds(row, ROWS, stride=PAIRS), :]
            b = sums[pl.ds(row + 1, ROWS, stride=PAIRS), :]
            for u, value in enumerate((jnp.where(low, a, swap_halves(b)), jnp.where(low, swap_halves(a), b))):
                hi = value.astype(BF)
                lo = (value - hi.astype(F32)).astype(BF)
                hi_ref[s, u, :, k * 128 : k * 128 + 128] = hi
                lo_ref[s, u, :, k * 128 : k * 128 + 128] = lo
        return carry

    lax.fori_loop(0, SLOTS, one, 0)


def weigh(counts, share):
    shape = jax.ShapeDtypeStruct((SLOTS, 2, ROWS, DEPTH), BF)
    tabs = TABS * SIDE * SIDE
    return pl.pallas_call(
        weigh_kernel,
        grid=(1,),
        in_specs=[
            pl.BlockSpec((tabs, PAIRS), lambda i: (0, 0)),
            pl.BlockSpec((tabs, SHARE), lambda i: (0, 0)),
        ],
        out_specs=[pl.BlockSpec(shape.shape, lambda i: (0, 0, 0, 0))] * 2,
        out_shape=[shape, shape],
        scratch_shapes=[pltpu.VMEM((ROWS * PAIRS, 128), F32)],
        compiler_params=pltpu.CompilerParams(vmem_limit_bytes=32 * MIB),
        name="weigh",
    )(counts, share)


def apply_kernel(meta, oh, ol, xh, xl, w0, w1, w2, w3, right, s0, s1, s2, s3, wave, lhs_hi, lhs_lo, total):
    core, x, y = meta[0], meta[1], meta[2]
    o = pl.program_id(0)

    @pl.when(o == 0)
    def _():
        for d, ref in enumerate((w0, w1, w2, w3)):
            place = pl.multiple_of(lax.rem(x - d + SIDE, SIDE) * ROWS, ROWS)
            wave[:, pl.ds(place, ROWS), :] = ref[...]

    weights = wave[...].reshape(DEPTH, WIDTH)
    mine = pl.multiple_of(core * ROWS, ROWS)
    theirs = pl.multiple_of((1 - core) * ROWS, ROWS)
    for half, hi_ref, lo_ref in ((mine, oh, ol), (theirs, xh, xl)):
        lhs_hi[:, pl.ds(half, ROWS), :] = hi_ref[...].reshape(4, ROWS, DEPTH)
        lhs_lo[:, pl.ds(half, ROWS), :] = lo_ref[...].reshape(4, ROWS, DEPTH)
    channel = jnp.dot(lhs_hi[...].reshape(128, DEPTH), weights, preferred_element_type=F32)
    channel = channel + jnp.dot(lhs_lo[...].reshape(128, DEPTH), weights, preferred_element_type=F32)
    hi = channel.astype(BF)
    lo = (channel - hi.astype(F32)).astype(BF)
    result = jnp.zeros((HALF, WIDTH), F32)
    for p in range(2):
        env = right[meta[3 + 2 * o + p]]
        rows = slice(p * HALF, (p + 1) * HALF)
        result = result + jnp.dot(hi[rows], env, preferred_element_type=F32)
        result = result + jnp.dot(lo[rows], env, preferred_element_type=F32)
    total[...] = result
    for d, ref in enumerate((s0, s1, s2, s3)):
        place = pl.multiple_of(lax.rem(y + d, SIDE) * ROWS, ROWS)
        ref[0] = total[pl.ds(place, ROWS), :]


def apply(meta, own, far, pieces, right):
    sectors = SLOTS // 2
    lhs_spec = pl.BlockSpec((2, 2, ROWS, DEPTH), lambda o, m: (o, 0, 0, 0))
    whole = lambda a: pl.BlockSpec(a.shape, lambda o, m: (0, 0, 0))
    return pl.pallas_call(
        apply_kernel,
        grid_spec=pltpu.PrefetchScalarGridSpec(
            num_scalar_prefetch=1,
            grid=(sectors,),
            in_specs=[lhs_spec] * 4 + [whole(p) for p in pieces] + [whole(right)],
            out_specs=[pl.BlockSpec((1, ROWS, WIDTH), lambda o, m: (o, 0, 0))] * 4,
            scratch_shapes=[
                pltpu.VMEM((PICKS, HALF, WIDTH), BF),
                pltpu.VMEM((4, 2 * ROWS, DEPTH), BF),
                pltpu.VMEM((4, 2 * ROWS, DEPTH), BF),
                pltpu.VMEM((HALF, WIDTH), F32),
            ],
        ),
        out_shape=[jax.ShapeDtypeStruct((sectors, ROWS, WIDTH), F32)] * 4,
        compiler_params=pltpu.CompilerParams(vmem_limit_bytes=32 * MIB),
        name="apply",
    )(meta, *own, *far, *pieces, right)


def along_table(dy, dx):
    return [
        (y * SIDE + x, (y + dy) % SIDE * SIDE + (x + dx) % SIDE) for y in range(SIDE) for x in range(SIDE)
    ]


def along_sector(dz, dc):
    return [(z * 2 + c, (z + dz) % SIDE * 2 + (c ^ dc)) for z in range(SIDE) for c in range(2)]


def local(
    wave_blocks,
    recoupling,
    right_blocks,
    sector_sizes,
    channel_env,
    fetch_list,
    term_pick,
    term_table,
    term_slot,
    term_live,
):
    sector = lax.axis_index("sector")
    place = lax.axis_index("table")
    z, core = sector // 2, sector % 2
    y, x = place // SIDE, place % SIDE

    other = lax.ppermute(wave_blocks, "sector", along_sector(0, 1))
    both = jnp.concatenate([wave_blocks, other], axis=0)
    pool = [both] + [lax.ppermute(both, "sector", along_sector(d, 0)) for d in (1, 2, 3)]

    terms = jnp.stack([term_slot * PICKS + term_pick, term_table, term_live])
    sent = pack(core.reshape(1), recoupling, terms)
    mine = lax.all_to_all(sent, "table", 0, 0).reshape(TABS * SIDE * SIDE, SENT)
    theirs = lax.ppermute(mine, "sector", along_sector(0, 1))

    chosen = select(jnp.concatenate([jnp.stack([z, core]), fetch_list.reshape(-1)]), pool)
    pieces = [chosen] + [lax.ppermute(chosen, "table", along_table(0, d)) for d in (1, 2, 3)]

    counts = mine[:, SHARE:]
    own = weigh(counts, mine)
    far = weigh(counts, theirs)
    meta = jnp.concatenate([jnp.stack([core, x, y]), channel_env.reshape(-1)])
    parts = apply(meta, own, far, pieces, right_blocks)
    result = parts[0]
    for d in (1, 2, 3):
        result = result + lax.ppermute(parts[d], "table", along_table(d, 0))

    rows = place * ROWS + jnp.arange(ROWS, dtype=jnp.int32)
    columns = jnp.arange(WIDTH, dtype=jnp.int32)
    limits = sector_sizes[:, None, None]
    keep = (rows[None, :, None] < limits) & (columns[None, None, :] < limits)
    return jnp.where(keep, result, jnp.float32(0.0))


def solution(mesh):
    placed = (
        P("sector", "table", None),
        P("table", None, None),
        P("sector", None, None),
        P("sector"),
        P("sector", None),
        P("sector", None, None),
        P(("sector", "table")),
        P(("sector", "table")),
        P(("sector", "table")),
        P(("sector", "table")),
    )
    return jax.shard_map(
        local, mesh=mesh, in_specs=placed, out_specs=P("sector", "table", None), check_vma=False
    )
```

```python
import functools

import jax
import jax.numpy as jnp
from jax import lax
from jax.experimental import pallas as pl
from jax.experimental.pallas import tpu as pltpu
from jax.sharding import PartitionSpec as P

BF = jnp.bfloat16
F32 = jnp.float32
SIDE = 4
TABS = 16
ROWS = 16
HALF = 64
WIDTH = 256
SLOTS = 16
PICKS = 24
PAIRS = SLOTS * PICKS
SHARE = ROWS * 128
SENT = SHARE + PAIRS
DEPTH = PICKS * HALF
PITCH = PAIRS + 8
MIB = 1 << 20
WEIGH_COST = 100_000_000_000


def swap_halves(value):
    return pltpu.roll(value, 64, 1)


def pack_kernel(meta, t0_ref, t1_ref, terms_ref, out_ref, rows0, rows1, count):
    low = lax.broadcasted_iota(jnp.int32, (TABS, 128), 1) < 64

    @pl.when(pl.program_id(0) == 0)
    def _():
        pair = terms_ref[0:1, :]
        tab = terms_ref[1:2, :]
        live = terms_ref[2:3, :]
        terms = terms_ref.shape[1]
        tab_hot = (lax.broadcasted_iota(jnp.int32, (TABS, terms), 0) == tab) & (live > 0)
        pair_hot = lax.broadcasted_iota(jnp.int32, (PAIRS, terms), 0) == pair
        counts = lax.dot_general(
            tab_hot.astype(F32).astype(BF),
            pair_hot.astype(F32).astype(BF),
            (((1,), (1,)), ((), ())),
            preferred_element_type=F32,
        )
        count[...] = counts.astype(BF)

    for k in range(2):
        rows0[k] = t0_ref[:, 0, :, k * 128 : k * 128 + 128].reshape(TABS * ROWS, 128).astype(F32)
        rows1[k] = t1_ref[:, 0, :, k * 128 : k * 128 + 128].reshape(TABS * ROWS, 128).astype(F32)
    for y in range(SIDE):
        out_ref[y, 0, :, SHARE:SENT] = count[...]
    for q in range(ROWS):
        lanes = slice(q * 128, q * 128 + 128)
        for k in range(2):
            a = rows0[k, pl.ds(q, TABS, stride=ROWS), :]
            b = rows1[k, pl.ds(q, TABS, stride=ROWS), :]
            out_ref[2 * k, 0, :, lanes] = jnp.where(low, a, swap_halves(b)).astype(BF)
            out_ref[2 * k + 1, 0, :, lanes] = jnp.where(low, swap_halves(a), b).astype(BF)


def pack(core, recoupling, terms):
    blocks = recoupling.reshape(TABS, SIDE, HALF, WIDTH)
    out = pl.pallas_call(
        pack_kernel,
        grid_spec=pltpu.PrefetchScalarGridSpec(
            num_scalar_prefetch=1,
            grid=(SIDE,),
            in_specs=[
                pl.BlockSpec((TABS, 1, ROWS, WIDTH), lambda x, m: (0, m[0], x, 0)),
                pl.BlockSpec((TABS, 1, ROWS, WIDTH), lambda x, m: (0, m[0] + 2, x, 0)),
                pl.BlockSpec(terms.shape, lambda x, m: (0, 0)),
            ],
            out_specs=pl.BlockSpec((SIDE, 1, TABS, SENT), lambda x, m: (0, x, 0, 0)),
            scratch_shapes=[
                pltpu.VMEM((2, TABS * ROWS, 128), F32),
                pltpu.VMEM((2, TABS * ROWS, 128), F32),
                pltpu.VMEM((TABS, PAIRS), BF),
            ],
        ),
        out_shape=jax.ShapeDtypeStruct((SIDE, SIDE, TABS, SENT), BF),
        compiler_params=pltpu.CompilerParams(vmem_limit_bytes=24 * MIB),
        name="pack",
    )(core, blocks, blocks, terms)
    return out.reshape(SIDE * SIDE, TABS, SENT)


def select_kernel(meta, w0, w1, w2, w3, out_ref):
    z = meta[0]
    core = meta[1]
    for p in range(PICKS):
        group = p // 3
        piece = meta[2 + p]
        step = lax.rem(z - group // 2 + SIDE, SIDE)
        other = jnp.where(core == group % 2, 0, 1)
        for d, ref in enumerate((w0, w1, w2, w3)):

            @pl.when(step == d)
            def _(ref=ref, p=p, other=other, piece=piece):
                out_ref[p] = ref[other * 8 + piece]


def select(meta, pieces):
    return pl.pallas_call(
        select_kernel,
        in_specs=[pl.BlockSpec(memory_space=pltpu.SMEM)] + [pl.BlockSpec(memory_space=pltpu.VMEM)] * 4,
        out_specs=pl.BlockSpec(memory_space=pltpu.VMEM),
        out_shape=jax.ShapeDtypeStruct((PICKS, ROWS, WIDTH), BF),
        compiler_params=pltpu.CompilerParams(vmem_limit_bytes=8 * MIB),
        name="select",
    )(meta, *pieces)


def weigh_kernel(c_ref, t_ref, hi_ref, lo_ref, sums):
    counts = c_ref[:, SHARE:SENT]
    for n in range(ROWS // 2):
        part = lax.dot_general(
            counts, t_ref[:, n * 256 : n * 256 + 256], (((0,), (0,)), ((), ())), preferred_element_type=F32
        )
        for k in range(2):
            start = (2 * n + k) * PITCH
            sums[start : start + PAIRS, :] = part[:, k * 128 : k * 128 + 128]
    low = lax.broadcasted_iota(jnp.int32, (ROWS, 128), 1) < 64

    def one(s, carry):
        for k in range(PICKS // 2):
            row = s * PICKS + 2 * k
            a = sums[pl.ds(row, ROWS, stride=PITCH), :]
            b = sums[pl.ds(row + 1, ROWS, stride=PITCH), :]
            for u, value in enumerate((jnp.where(low, a, swap_halves(b)), jnp.where(low, swap_halves(a), b))):
                hi = value.astype(BF)
                lo = (value - hi.astype(F32)).astype(BF)
                place = pl.ds(pl.multiple_of((2 * s + u) * ROWS, ROWS), ROWS)
                hi_ref[place, k * 128 : k * 128 + 128] = hi
                lo_ref[place, k * 128 : k * 128 + 128] = lo
        return carry

    lax.fori_loop(0, SLOTS, one, 0, unroll=4)


def weigh(counts, share):
    shape = jax.ShapeDtypeStruct((SLOTS * 2 * ROWS, DEPTH), BF)
    here = pl.BlockSpec(memory_space=pltpu.VMEM)
    return pl.pallas_call(
        weigh_kernel,
        in_specs=[here, here],
        out_specs=[here, here],
        out_shape=[shape, shape],
        scratch_shapes=[pltpu.VMEM((ROWS * PITCH, 128), F32)],
        compiler_params=pltpu.CompilerParams(vmem_limit_bytes=24 * MIB),
        cost_estimate=pl.CostEstimate(flops=WEIGH_COST, bytes_accessed=8 * MIB, transcendentals=0),
        name="weigh",
    )(counts, share)


def apply_kernel(meta, oh, ol, xh, xl, w0, w1, w2, w3, right, s0, s1, s2, s3, wave, channel, total):
    core, x, y = meta[0], meta[1], meta[2]
    for d, ref in enumerate((w0, w1, w2, w3)):
        place = pl.multiple_of(lax.rem(x - d + SIDE, SIDE) * ROWS, ROWS)
        wave[:, pl.ds(place, ROWS), :] = ref[...]
    weights = wave[...].reshape(DEPTH, WIDTH)
    for half, (hi_ref, lo_ref) in enumerate(((oh, ol), (xh, xl))):
        part = jnp.dot(hi_ref[...], weights, preferred_element_type=F32)
        channel[half] = part + jnp.dot(lo_ref[...], weights, preferred_element_type=F32)
    step = 2 * ROWS
    for o in range(SLOTS // 2):
        result = jnp.zeros((HALF, WIDTH), F32)
        for s in (2 * o, 2 * o + 1):
            env = right[meta[3 + s]]
            value = jnp.concatenate([channel[half, s * step : (s + 1) * step] for half in range(2)], axis=0)
            hi = value.astype(BF)
            lo = (value - hi.astype(F32)).astype(BF)
            part = jnp.dot(jnp.concatenate([hi, lo], axis=0), env, preferred_element_type=F32)
            result = result + (part[:HALF] + part[HALF:])
        for half in range(2):
            for u in range(2):
                owner = 2 * u + (core if half == 0 else 1 - core)
                total[owner, o] = result[(2 * half + u) * ROWS : (2 * half + u + 1) * ROWS]
    for d, ref in enumerate((s0, s1, s2, s3)):
        ref[...] = total[lax.rem(y + d, SIDE)]


def apply(meta, own, far, pieces, right):
    sectors = SLOTS // 2
    here = pl.BlockSpec(memory_space=pltpu.VMEM)
    return pl.pallas_call(
        apply_kernel,
        in_specs=[pl.BlockSpec(memory_space=pltpu.SMEM)] + [here] * 9,
        out_specs=[here] * 4,
        out_shape=[jax.ShapeDtypeStruct((sectors, ROWS, WIDTH), F32)] * 4,
        scratch_shapes=[
            pltpu.VMEM((PICKS, HALF, WIDTH), BF),
            pltpu.VMEM((2, SLOTS * 2 * ROWS, WIDTH), F32),
            pltpu.VMEM((SIDE, sectors, ROWS, WIDTH), F32),
        ],
        compiler_params=pltpu.CompilerParams(vmem_limit_bytes=24 * MIB),
        name="apply",
    )(meta, *own, *far, *pieces, right)


def along_table(dy, dx):
    return [
        (y * SIDE + x, (y + dy) % SIDE * SIDE + (x + dx) % SIDE) for y in range(SIDE) for x in range(SIDE)
    ]


def along_sector(dz, dc):
    return [(z * 2 + c, (z + dz) % SIDE * 2 + (c ^ dc)) for z in range(SIDE) for c in range(2)]


def local(
    wave_blocks,
    recoupling,
    right_blocks,
    sector_sizes,
    channel_env,
    fetch_list,
    term_pick,
    term_table,
    term_slot,
    term_live,
):
    sector = lax.axis_index("sector")
    place = lax.axis_index("table")
    z, core = sector // 2, sector % 2
    y, x = place // SIDE, place % SIDE

    other = lax.ppermute(wave_blocks, "sector", along_sector(0, 1))
    both = jnp.concatenate([wave_blocks, other], axis=0)
    terms = jnp.stack([term_slot * PICKS + term_pick, term_table, term_live])
    sent = pack(core.reshape(1), recoupling, terms)
    sent, both = lax.optimization_barrier((sent, both))
    mine = lax.all_to_all(sent, "table", 0, 0).reshape(TABS * SIDE * SIDE, SENT)
    theirs = lax.ppermute(mine, "sector", along_sector(0, 1))

    pool = [both] + [lax.ppermute(both, "sector", along_sector(d, 0)) for d in (1, 2, 3)]
    chosen = select(jnp.concatenate([jnp.stack([z, core]), fetch_list.reshape(-1)]), pool)
    pieces = [chosen] + [lax.ppermute(chosen, "table", along_table(0, d)) for d in (1, 2, 3)]

    own = weigh(mine, mine)
    far = weigh(mine, theirs)
    meta = jnp.concatenate([jnp.stack([core, x, y]), channel_env.reshape(-1)])
    parts = apply(meta, own, far, pieces, right_blocks)
    result = parts[0]
    for d in (1, 2, 3):
        result = result + lax.ppermute(parts[d], "table", along_table(d, 0))

    rows = place * ROWS + jnp.arange(ROWS, dtype=jnp.int32)
    columns = jnp.arange(WIDTH, dtype=jnp.int32)
    limits = sector_sizes[:, None, None]
    keep = (rows[None, :, None] < limits) & (columns[None, None, :] < limits)
    return jnp.where(keep, result, jnp.float32(0.0))


def solution(mesh):
    placed = (
        P("sector", "table", None),
        P("table", None, None),
        P("sector", None, None),
        P("sector"),
        P("sector", None),
        P("sector", None, None),
        P(("sector", "table")),
        P(("sector", "table")),
        P(("sector", "table")),
        P(("sector", "table")),
    )
    return jax.shard_map(
        local, mesh=mesh, in_specs=placed, out_specs=P("sector", "table", None), check_vma=False
    )
```

```python
import functools

import jax
import jax.numpy as jnp
from jax import lax
from jax.experimental import pallas as pl
from jax.experimental.pallas import tpu as pltpu
from jax.sharding import PartitionSpec as P

BF = jnp.bfloat16
F32 = jnp.float32
SIDE = 4
TABS = 16
ROWS = 16
HALF = 64
WIDTH = 256
SLOTS = 16
PICKS = 24
PAIRS = SLOTS * PICKS
SHARE = ROWS * 128
SENT = SHARE + PAIRS
DEPTH = PICKS * HALF
PITCH = PAIRS + 8
ROW_PITCH = ROWS + 8
PACK_MIB = 16
MIB = 1 << 20
ENV = 4
SIZE = ENV + SLOTS
FETCH = SIZE + SLOTS // 2
LISTED = 3
STEP = SLOTS * ROWS
X_ORDER = (2, 1, 3)
Z_ORDER = (2, 1, 3)
PLANES = (0, 2, 1, 3)
CHOOSE_COST = 1_000_000_000
OWN_COST = 100_000_000_000
FAR_COST = 4_000_000_000
WEIGH_COST = 100_000_000_000


def in_hbm(value):
    return pltpu.with_memory_space_constraint(value, pltpu.HBM)


def swap_halves(value):
    return pltpu.roll(value, 64, 1)


def pack_kernel(meta, blocks, pick_in, tab_in, slot_in, live_in, out_ref, held, lists, rows, ready, sems, list_sems, out_sems):
    core = meta[0]

    def fetch(x, u):
        source = blocks.at[:, core + 2 * u, pl.ds(x * ROWS, ROWS), :]
        return pltpu.make_async_copy(source, held.at[x, u], sems.at[x, u])

    def hand(x):
        return pltpu.make_async_copy(ready.at[x], out_ref.at[:, x], out_sems.at[x])

    copies = []
    for n, ref in enumerate((pick_in, tab_in, slot_in, live_in)):
        copies.append(pltpu.make_async_copy(ref, lists.at[n], list_sems.at[n]))
        copies[n].start()
    for x in range(SIDE):
        for u in range(2):
            fetch(x, u).start()
    for copy in copies:
        copy.wait()

    terms = pick_in.shape[1]
    tab_hot = (lax.broadcasted_iota(jnp.int32, (TABS, terms), 0) == lists[1]) & (lists[3] > 0)
    pair = lists[2] * PICKS + lists[0]
    pair_hot = lax.broadcasted_iota(jnp.int32, (PAIRS, terms), 0) == pair
    counts = lax.dot_general(
        tab_hot.astype(F32).astype(BF),
        pair_hot.astype(F32).astype(BF),
        (((1,), (1,)), ((), ())),
        preferred_element_type=F32,
    ).astype(BF)
    for y in range(SIDE):
        for x in range(SIDE):
            ready[x, y, :, SHARE:SENT] = counts

    low = lax.broadcasted_iota(jnp.int32, (TABS, 128), 1) < 64
    for x in range(SIDE):
        for u in range(2):
            fetch(x, u).wait()
            for t in range(TABS):
                block = held[x, u, t].astype(F32)
                for k in range(2):
                    rows[k, u, t * ROW_PITCH : t * ROW_PITCH + ROWS, :] = block[:, k * 128 : k * 128 + 128]
        for q in range(ROWS):
            lanes = slice(q * 128, q * 128 + 128)
            for k in range(2):
                a = rows[k, 0, pl.ds(q, TABS, stride=ROW_PITCH), :]
                b = rows[k, 1, pl.ds(q, TABS, stride=ROW_PITCH), :]
                mixed = swap_halves(jnp.where(low, b, a))
                ready[x, 2 * k, :, lanes] = jnp.where(low, a, mixed).astype(BF)
                ready[x, 2 * k + 1, :, lanes] = jnp.where(low, mixed, b).astype(BF)
        hand(x).start()
    for x in range(SIDE):
        hand(x).wait()


def pack(meta, recoupling, pick, tab, slot, live):
    there = pl.BlockSpec(memory_space=pltpu.HBM)
    out = pl.pallas_call(
        pack_kernel,
        in_specs=[pl.BlockSpec(memory_space=pltpu.SMEM)] + [there] * 5,
        out_specs=there,
        out_shape=pltpu.HBM((SIDE, SIDE, TABS, SENT), BF),
        scratch_shapes=[
            pltpu.VMEM((SIDE, 2, TABS, ROWS, WIDTH), BF),
            pltpu.VMEM((4, 1, pick.shape[0]), jnp.int32),
            pltpu.VMEM((2, 2, TABS * ROW_PITCH, 128), F32),
            pltpu.VMEM((SIDE, SIDE, TABS, SENT), BF),
            pltpu.SemaphoreType.DMA((SIDE, 2)),
            pltpu.SemaphoreType.DMA((4,)),
            pltpu.SemaphoreType.DMA((SIDE,)),
        ],
        compiler_params=pltpu.CompilerParams(vmem_limit_bytes=PACK_MIB * MIB),
        name="pack",
    )(
        meta,
        in_hbm(recoupling.reshape(TABS, SIDE, HALF, WIDTH)),
        *(in_hbm(v.reshape(1, -1)) for v in (pick, tab, slot, live)),
    )
    return out.reshape(SIDE * SIDE, TABS, SENT)


def spread(counts_ref, share_ref, sums, hi_ref, lo_ref):
    counts = counts_ref[:, SHARE:SENT]
    for n in range(ROWS // 2):
        part = lax.dot_general(
            counts, share_ref[:, n * 256 : n * 256 + 256], (((0,), (0,)), ((), ())), preferred_element_type=F32
        )
        for k in range(2):
            start = (2 * n + k) * PITCH
            sums[start : start + PAIRS, :] = part[:, k * 128 : k * 128 + 128]
    low = lax.broadcasted_iota(jnp.int32, (ROWS, 128), 1) < 64

    def one(s, carry):
        for k in range(PICKS // 2):
            row = s * PICKS + 2 * k
            a = sums[pl.ds(row, ROWS, stride=PITCH), :]
            b = sums[pl.ds(row + 1, ROWS, stride=PITCH), :]
            mixed = swap_halves(jnp.where(low, b, a))
            for u, value in enumerate((jnp.where(low, a, mixed), jnp.where(low, mixed, b))):
                hi = value.astype(BF)
                place = pl.ds(pl.multiple_of(u * STEP + s * ROWS, ROWS), ROWS)
                hi_ref[place, k * 128 : k * 128 + 128] = hi
                lo_ref[place, k * 128 : k * 128 + 128] = (value - hi.astype(F32)).astype(BF)
        return carry

    lax.fori_loop(0, SLOTS, one, 0, unroll=4)


def product(hi_ref, lo_ref, wave):
    part = jnp.dot(hi_ref[...], wave[...], preferred_element_type=F32)
    return part + jnp.dot(lo_ref[...], wave[...], preferred_element_type=F32)


def multiply(hi_ref, lo_ref, weights):
    part = jnp.dot(hi_ref[...], weights, preferred_element_type=F32)
    return part + jnp.dot(lo_ref[...], weights, preferred_element_type=F32)


def own_kernel(mine, hi_ref, lo_ref, sums):
    spread(mine, mine, sums, hi_ref, lo_ref)


def own_half(mine):
    here = pl.BlockSpec(memory_space=pltpu.VMEM)
    return pl.pallas_call(
        own_kernel,
        in_specs=[here],
        out_specs=[here] * 2,
        out_shape=[pltpu.VMEM((2 * STEP, DEPTH), BF)] * 2,
        scratch_shapes=[pltpu.VMEM((ROWS * PITCH, 128), F32)],
        compiler_params=pltpu.CompilerParams(vmem_limit_bytes=16 * MIB),
        cost_estimate=pl.CostEstimate(flops=OWN_COST, bytes_accessed=MIB, transcendentals=0),
        name="own_half",
    )(mine)


def choose_kernel(meta, hi_ref, lo_ref, *refs):
    planes, (out_ref, wave) = refs[:8], refs[8:]
    core, x, z = meta[0], meta[1], meta[3]
    for c in range(2):
        for place, e in enumerate(PLANES):
            group = 2 * lax.rem(z - e + SIDE, SIDE) + (core if c == 0 else 1 - core)
            for n in range(LISTED):
                pick = LISTED * group + n
                piece = meta[FETCH + pick]
                for d in range(SIDE):
                    rows = pl.ds(pl.multiple_of(lax.rem(x - d + SIDE, SIDE) * ROWS, ROWS), ROWS)
                    wave[pick, rows, :] = planes[c * SIDE + place][d, piece]
    out_ref[...] = multiply(hi_ref, lo_ref, wave[...].reshape(DEPTH, WIDTH))


def choose(meta, own, planes):
    here = pl.BlockSpec(memory_space=pltpu.VMEM)
    return pl.pallas_call(
        choose_kernel,
        in_specs=[pl.BlockSpec(memory_space=pltpu.SMEM)] + [here] * 10,
        out_specs=[here] * 2,
        out_shape=[pltpu.VMEM((2 * STEP, WIDTH), F32), pltpu.VMEM((PICKS, HALF, WIDTH), BF)],
        compiler_params=pltpu.CompilerParams(vmem_limit_bytes=16 * MIB),
        cost_estimate=pl.CostEstimate(flops=CHOOSE_COST, bytes_accessed=MIB, transcendentals=0),
        name="choose",
    )(meta, *own, *planes)


def far_kernel(meta, mine, theirs, own, wave, right, s0, s1, s2, s3, sums, hi_ref, lo_ref, channel):
    core, x, y = meta[0], meta[1], meta[2]
    spread(mine, theirs, sums, hi_ref, lo_ref)
    weights = wave[...].reshape(DEPTH, WIDTH)
    for u in range(2):
        rows = slice(u * STEP, (u + 1) * STEP)
        channel[lax.rem(2 * u + core - y + SIDE, SIDE)] = own[rows, :]
        part = jnp.dot(hi_ref[rows, :], weights, preferred_element_type=F32)
        part = part + jnp.dot(lo_ref[rows, :], weights, preferred_element_type=F32)
        channel[lax.rem(2 * u + 1 - core - y + SIDE, SIDE)] = part
    columns = lax.broadcasted_iota(jnp.int32, (ROWS, WIDTH), 1)
    lines = lax.broadcasted_iota(jnp.int32, (ROWS, WIDTH), 0)
    reach = [jnp.maximum(lines + (lax.rem(y + d, SIDE) * SIDE + x) * ROWS, columns) for d in range(SIDE)]
    for o in range(SLOTS // 2):
        result = None
        for s in (2 * o, 2 * o + 1):
            env = right[meta[ENV + s]]
            value = channel[:, s * ROWS : (s + 1) * ROWS, :].reshape(HALF, WIDTH)
            hi = value.astype(BF)
            lo = (value - hi.astype(F32)).astype(BF)
            part = jnp.dot(jnp.concatenate([hi, lo], axis=0), env, preferred_element_type=F32)
            part = part[:HALF] + part[HALF:]
            result = part if result is None else result + part
        size = meta[SIZE + o]
        for d, ref in enumerate((s0, s1, s2, s3)):
            ref[o] = jnp.where(reach[d] < size, result[d * ROWS : (d + 1) * ROWS], 0.0)


def far_half(meta, mine, theirs, own, wave, right):
    sectors = SLOTS // 2
    here = pl.BlockSpec(memory_space=pltpu.VMEM)
    return pl.pallas_call(
        far_kernel,
        in_specs=[pl.BlockSpec(memory_space=pltpu.SMEM)] + [here] * 5,
        out_specs=[here] * 4,
        out_shape=[pltpu.VMEM((sectors, ROWS, WIDTH), F32)] * 4,
        scratch_shapes=[
            pltpu.VMEM((ROWS * PITCH, 128), F32),
            pltpu.VMEM((2 * STEP, DEPTH), BF),
            pltpu.VMEM((2 * STEP, DEPTH), BF),
            pltpu.VMEM((SIDE, STEP, WIDTH), F32),
        ],
        compiler_params=pltpu.CompilerParams(vmem_limit_bytes=24 * MIB),
        cost_estimate=pl.CostEstimate(flops=FAR_COST, bytes_accessed=MIB, transcendentals=0),
        name="far_half",
    )(meta, mine, theirs, own, wave, right)


def along_table(dy, dx):
    return [
        (y * SIDE + x, (y + dy) % SIDE * SIDE + (x + dx) % SIDE) for y in range(SIDE) for x in range(SIDE)
    ]


def along_sector(dz, dc):
    return [(z * 2 + c, (z + dz) % SIDE * 2 + (c ^ dc)) for z in range(SIDE) for c in range(2)]


def local(
    wave_blocks,
    recoupling,
    right_blocks,
    sector_sizes,
    channel_env,
    fetch_list,
    term_pick,
    term_table,
    term_slot,
    term_live,
):
    sector = lax.axis_index("sector")
    place = lax.axis_index("table")
    z, core = sector // 2, sector % 2
    y, x = place // SIDE, place % SIDE

    meta = jnp.concatenate(
        [jnp.stack([core, x, y, z]), channel_env.reshape(-1), sector_sizes, fetch_list.reshape(-1)]
    )

    lines = {0: wave_blocks}
    for d in X_ORDER:
        lines[d] = lax.ppermute(wave_blocks, "table", along_table(0, d))
    lines = [lines[d] for d in range(SIDE)]
    sent = pack(core.reshape(1), recoupling, term_pick, term_table, term_slot, term_live)
    sent, lines = lax.optimization_barrier((sent, lines))
    mine = lax.all_to_all(sent, "table", 0, 0).reshape(TABS * SIDE * SIDE, SENT)
    theirs = lax.ppermute(mine, "sector", along_sector(0, 1))

    planes = {0: jnp.stack(lines)}
    for e in Z_ORDER:
        planes[e] = lax.ppermute(planes[0], "sector", along_sector(e, 0))
    planes = [planes[e] for e in PLANES]
    planes = planes + [lax.ppermute(p, "sector", along_sector(0, 1)) for p in planes]
    own, wave = choose(meta, own_half(mine), planes)
    parts = far_half(meta, mine, theirs, own, wave, right_blocks)
    result = parts[0]
    for d in (2, 1, 3):
        result = result + lax.ppermute(parts[d], "table", along_table(d, 0))
    return result


def solution(mesh):
    placed = (
        P("sector", "table", None),
        P("table", None, None),
        P("sector", None, None),
        P("sector"),
        P("sector", None),
        P("sector", None, None),
        P(("sector", "table")),
        P(("sector", "table")),
        P(("sector", "table")),
        P(("sector", "table")),
    )
    return jax.shard_map(
        local, mesh=mesh, in_specs=placed, out_specs=P("sector", "table", None), check_vma=False
    )
```

```python
import functools

import jax
import jax.numpy as jnp
from jax import lax
from jax.experimental import pallas as pl
from jax.experimental.pallas import tpu as pltpu
from jax.sharding import PartitionSpec as P

BF = jnp.bfloat16
F32 = jnp.float32
SIDE = 4
TABS = 16
ROWS = 16
HALF = 64
WIDTH = 256
SLOTS = 16
PICKS = 24
PAIRS = SLOTS * PICKS
SHARE = ROWS * 128
SENT = SHARE + PAIRS
DEPTH = PICKS * HALF
PITCH = PAIRS + 8
ROW_PITCH = ROWS + 8
PACK_MIB = 16
MIB = 1 << 20
ENV = 4
SIZE = ENV + SLOTS
FETCH = SIZE + SLOTS // 2
LISTED = 3
LIMIT = 32700.0
STEP = SLOTS * ROWS
X_ORDER = (2, 1, 3)
Z_ORDER = (2, 1, 3)
PLANES = (0, 2, 1, 3)
CHOOSE_COST = 1_000_000_000
OWN_COST = 100_000_000_000
FAR_COST = 4_000_000_000
WEIGH_COST = 100_000_000_000


def in_hbm(value):
    return pltpu.with_memory_space_constraint(value, pltpu.HBM)


def swap_halves(value):
    return pltpu.roll(value, 64, 1)


def pack_kernel(meta, blocks, pick_in, tab_in, slot_in, live_in, out_ref, held, lists, rows, ready, sems, list_sems, out_sems):
    core = meta[0]

    def fetch(x, u):
        source = blocks.at[:, core + 2 * u, pl.ds(x * ROWS, ROWS), :]
        return pltpu.make_async_copy(source, held.at[x, u], sems.at[x, u])

    def hand(x):
        return pltpu.make_async_copy(ready.at[x], out_ref.at[:, x], out_sems.at[x])

    copies = []
    for n, ref in enumerate((pick_in, tab_in, slot_in, live_in)):
        copies.append(pltpu.make_async_copy(ref, lists.at[n], list_sems.at[n]))
        copies[n].start()
    for x in range(SIDE):
        for u in range(2):
            fetch(x, u).start()
    for copy in copies:
        copy.wait()

    terms = pick_in.shape[1]
    tab_hot = (lax.broadcasted_iota(jnp.int32, (TABS, terms), 0) == lists[1]) & (lists[3] > 0)
    pair = lists[2] * PICKS + lists[0]
    pair_hot = lax.broadcasted_iota(jnp.int32, (PAIRS, terms), 0) == pair
    counts = lax.dot_general(
        tab_hot.astype(F32).astype(BF),
        pair_hot.astype(F32).astype(BF),
        (((1,), (1,)), ((), ())),
        preferred_element_type=F32,
    ).astype(BF)
    for y in range(SIDE):
        for x in range(SIDE):
            ready[x, y, :, SHARE:SENT] = counts

    low = lax.broadcasted_iota(jnp.int32, (TABS, 128), 1) < 64
    for x in range(SIDE):
        for u in range(2):
            fetch(x, u).wait()
            for t in range(TABS):
                block = held[x, u, t].astype(F32)
                for k in range(2):
                    rows[k, u, t * ROW_PITCH : t * ROW_PITCH + ROWS, :] = block[:, k * 128 : k * 128 + 128]
        for q in range(ROWS):
            lanes = slice(q * 128, q * 128 + 128)
            for k in range(2):
                a = rows[k, 0, pl.ds(q, TABS, stride=ROW_PITCH), :]
                b = rows[k, 1, pl.ds(q, TABS, stride=ROW_PITCH), :]
                mixed = swap_halves(jnp.where(low, b, a))
                ready[x, 2 * k, :, lanes] = jnp.where(low, a, mixed).astype(BF)
                ready[x, 2 * k + 1, :, lanes] = jnp.where(low, mixed, b).astype(BF)
        hand(x).start()
    for x in range(SIDE):
        hand(x).wait()


def pack(meta, recoupling, pick, tab, slot, live):
    there = pl.BlockSpec(memory_space=pltpu.HBM)
    out = pl.pallas_call(
        pack_kernel,
        in_specs=[pl.BlockSpec(memory_space=pltpu.SMEM)] + [there] * 5,
        out_specs=there,
        out_shape=pltpu.HBM((SIDE, SIDE, TABS, SENT), BF),
        scratch_shapes=[
            pltpu.VMEM((SIDE, 2, TABS, ROWS, WIDTH), BF),
            pltpu.VMEM((4, 1, pick.shape[0]), jnp.int32),
            pltpu.VMEM((2, 2, TABS * ROW_PITCH, 128), F32),
            pltpu.VMEM((SIDE, SIDE, TABS, SENT), BF),
            pltpu.SemaphoreType.DMA((SIDE, 2)),
            pltpu.SemaphoreType.DMA((4,)),
            pltpu.SemaphoreType.DMA((SIDE,)),
        ],
        compiler_params=pltpu.CompilerParams(vmem_limit_bytes=PACK_MIB * MIB),
        name="pack",
    )(
        meta,
        in_hbm(recoupling.reshape(TABS, SIDE, HALF, WIDTH)),
        *(in_hbm(v.reshape(1, -1)) for v in (pick, tab, slot, live)),
    )
    return out.reshape(SIDE * SIDE, TABS, SENT)


def spread(counts_ref, share_ref, sums, hi_ref, lo_ref):
    counts = counts_ref[:, SHARE:SENT]
    for n in range(ROWS // 2):
        part = lax.dot_general(
            counts, share_ref[:, n * 256 : n * 256 + 256], (((0,), (0,)), ((), ())), preferred_element_type=F32
        )
        for k in range(2):
            start = (2 * n + k) * PITCH
            sums[start : start + PAIRS, :] = part[:, k * 128 : k * 128 + 128]
    low = lax.broadcasted_iota(jnp.int32, (ROWS, 128), 1) < 64

    def one(s, carry):
        for k in range(PICKS // 2):
            row = s * PICKS + 2 * k
            a = sums[pl.ds(row, ROWS, stride=PITCH), :]
            b = sums[pl.ds(row + 1, ROWS, stride=PITCH), :]
            mixed = swap_halves(jnp.where(low, b, a))
            for u, value in enumerate((jnp.where(low, a, mixed), jnp.where(low, mixed, b))):
                hi = value.astype(BF)
                place = pl.ds(pl.multiple_of(u * STEP + s * ROWS, ROWS), ROWS)
                hi_ref[place, k * 128 : k * 128 + 128] = hi
                lo_ref[place, k * 128 : k * 128 + 128] = (value - hi.astype(F32)).astype(BF)
        return carry

    lax.fori_loop(0, SLOTS, one, 0, unroll=4)


def product(hi_ref, lo_ref, wave):
    part = jnp.dot(hi_ref[...], wave[...], preferred_element_type=F32)
    return part + jnp.dot(lo_ref[...], wave[...], preferred_element_type=F32)


def multiply(hi_ref, lo_ref, weights):
    part = jnp.dot(hi_ref[...], weights, preferred_element_type=F32)
    return part + jnp.dot(lo_ref[...], weights, preferred_element_type=F32)


def own_kernel(mine, hi_ref, lo_ref, sums):
    spread(mine, mine, sums, hi_ref, lo_ref)


def own_half(mine):
    here = pl.BlockSpec(memory_space=pltpu.VMEM)
    return pl.pallas_call(
        own_kernel,
        in_specs=[here],
        out_specs=[here] * 2,
        out_shape=[pltpu.VMEM((2 * STEP, DEPTH), BF)] * 2,
        scratch_shapes=[pltpu.VMEM((ROWS * PITCH, 128), F32)],
        compiler_params=pltpu.CompilerParams(vmem_limit_bytes=16 * MIB),
        cost_estimate=pl.CostEstimate(flops=OWN_COST, bytes_accessed=MIB, transcendentals=0),
        name="own_half",
    )(mine)


def choose_kernel(meta, hi_ref, lo_ref, *refs):
    planes, (out_ref, wave) = refs[:8], refs[8:]
    core, x, z = meta[0], meta[1], meta[3]
    for c in range(2):
        for place, e in enumerate(PLANES):
            group = 2 * lax.rem(z - e + SIDE, SIDE) + (core if c == 0 else 1 - core)
            for n in range(LISTED):
                pick = LISTED * group + n
                piece = meta[FETCH + pick]
                for d in range(SIDE):
                    rows = pl.ds(pl.multiple_of(lax.rem(x - d + SIDE, SIDE) * ROWS, ROWS), ROWS)
                    wave[pick, rows, :] = planes[c * SIDE + place][d, piece]
    out_ref[...] = multiply(hi_ref, lo_ref, wave[...].reshape(DEPTH, WIDTH))


def choose(meta, own, planes):
    here = pl.BlockSpec(memory_space=pltpu.VMEM)
    return pl.pallas_call(
        choose_kernel,
        in_specs=[pl.BlockSpec(memory_space=pltpu.SMEM)] + [here] * 10,
        out_specs=[here] * 2,
        out_shape=[pltpu.VMEM((2 * STEP, WIDTH), F32), pltpu.VMEM((PICKS, HALF, WIDTH), BF)],
        compiler_params=pltpu.CompilerParams(vmem_limit_bytes=16 * MIB),
        cost_estimate=pl.CostEstimate(flops=CHOOSE_COST, bytes_accessed=MIB, transcendentals=0),
        name="choose",
    )(meta, *own, *planes)


def far_kernel(meta, mine, theirs, own, wave, right, s0, s1, s2, s3, sums, hi_ref, lo_ref, channel, codes):
    core, x, y = meta[0], meta[1], meta[2]
    codes[...] = jnp.zeros_like(codes)
    spread(mine, theirs, sums, hi_ref, lo_ref)
    weights = wave[...].reshape(DEPTH, WIDTH)
    for u in range(2):
        rows = slice(u * STEP, (u + 1) * STEP)
        channel[lax.rem(2 * u + core - y + SIDE, SIDE)] = own[rows, :]
        part = jnp.dot(hi_ref[rows, :], weights, preferred_element_type=F32)
        part = part + jnp.dot(lo_ref[rows, :], weights, preferred_element_type=F32)
        channel[lax.rem(2 * u + 1 - core - y + SIDE, SIDE)] = part
    columns = lax.broadcasted_iota(jnp.int32, (ROWS, WIDTH), 1)
    lines = lax.broadcasted_iota(jnp.int32, (ROWS, WIDTH), 0)
    reach = [jnp.maximum(lines + (lax.rem(y + d, SIDE) * SIDE + x) * ROWS, columns) for d in range(SIDE)]
    for o in range(SLOTS // 2):
        result = None
        for s in (2 * o, 2 * o + 1):
            env = right[meta[ENV + s]]
            value = channel[:, s * ROWS : (s + 1) * ROWS, :].reshape(HALF, WIDTH)
            hi = value.astype(BF)
            lo = (value - hi.astype(F32)).astype(BF)
            part = jnp.dot(jnp.concatenate([hi, lo], axis=0), env, preferred_element_type=F32)
            part = part[:HALF] + part[HALF:]
            result = part if result is None else result + part
        size = meta[SIZE + o]
        for d, ref in enumerate((s0, s1, s2, s3)):
            part = jnp.where(reach[d] < size, result[d * ROWS : (d + 1) * ROWS], 0.0)
            if d == 0:
                ref[o] = part
                continue
            peak = jnp.max(jnp.abs(part), axis=0, keepdims=True)
            code = jnp.ceil(jnp.log2(jnp.maximum(peak, 1e-30)) * 8.0 + 0.01)
            scaled = part * (jnp.exp2(code * -0.125) * LIMIT)
            ref[o] = jnp.round(scaled).astype(jnp.int32).astype(jnp.int16)
            codes[d - 1, o : o + 1, :] = code
    for d, ref in enumerate((s1, s2, s3)):
        ref[SLOTS // 2] = codes[d].astype(jnp.int32).astype(jnp.int16)


def far_half(meta, mine, theirs, own, wave, right):
    sectors = SLOTS // 2
    here = pl.BlockSpec(memory_space=pltpu.VMEM)
    return pl.pallas_call(
        far_kernel,
        in_specs=[pl.BlockSpec(memory_space=pltpu.SMEM)] + [here] * 5,
        out_specs=[here] * 4,
        out_shape=[pltpu.VMEM((sectors, ROWS, WIDTH), F32)] + [pltpu.VMEM((sectors + 1, ROWS, WIDTH), jnp.int16)] * 3,
        scratch_shapes=[
            pltpu.VMEM((ROWS * PITCH, 128), F32),
            pltpu.VMEM((2 * STEP, DEPTH), BF),
            pltpu.VMEM((2 * STEP, DEPTH), BF),
            pltpu.VMEM((SIDE, STEP, WIDTH), F32),
            pltpu.VMEM((3, ROWS, WIDTH), F32),
        ],
        compiler_params=pltpu.CompilerParams(vmem_limit_bytes=24 * MIB),
        cost_estimate=pl.CostEstimate(flops=FAR_COST, bytes_accessed=MIB, transcendentals=0),
        name="far_half",
    )(meta, mine, theirs, own, wave, right)


def finish_kernel(own, *refs):
    parts, out_ref = refs[:-1], refs[-1]
    scales = [jnp.exp2(ref[SLOTS // 2].astype(jnp.int32).astype(F32) * 0.125) * (1.0 / LIMIT) for ref in parts]
    for o in range(SLOTS // 2):
        total = own[o]
        for ref, scale in zip(parts, scales):
            total = total + ref[o].astype(jnp.int32).astype(F32) * scale[o : o + 1]
        out_ref[o] = total


def finish(own, parts):
    here = pl.BlockSpec(memory_space=pltpu.VMEM)
    return pl.pallas_call(
        finish_kernel,
        in_specs=[here] * 4,
        out_specs=here,
        out_shape=jax.ShapeDtypeStruct(own.shape, F32),
        compiler_params=pltpu.CompilerParams(vmem_limit_bytes=4 * MIB),
        name="finish",
    )(own, *parts)


def along_table(dy, dx):
    return [
        (y * SIDE + x, (y + dy) % SIDE * SIDE + (x + dx) % SIDE) for y in range(SIDE) for x in range(SIDE)
    ]


def along_sector(dz, dc):
    return [(z * 2 + c, (z + dz) % SIDE * 2 + (c ^ dc)) for z in range(SIDE) for c in range(2)]


def local(
    wave_blocks,
    recoupling,
    right_blocks,
    sector_sizes,
    channel_env,
    fetch_list,
    term_pick,
    term_table,
    term_slot,
    term_live,
):
    sector = lax.axis_index("sector")
    place = lax.axis_index("table")
    z, core = sector // 2, sector % 2
    y, x = place // SIDE, place % SIDE

    meta = jnp.concatenate(
        [jnp.stack([core, x, y, z]), channel_env.reshape(-1), sector_sizes, fetch_list.reshape(-1)]
    )

    lines = {0: wave_blocks}
    for d in X_ORDER:
        lines[d] = lax.ppermute(wave_blocks, "table", along_table(0, d))
    lines = [lines[d] for d in range(SIDE)]
    sent = pack(core.reshape(1), recoupling, term_pick, term_table, term_slot, term_live)
    sent, lines = lax.optimization_barrier((sent, lines))
    mine = lax.all_to_all(sent, "table", 0, 0).reshape(TABS * SIDE * SIDE, SENT)
    theirs = lax.ppermute(mine, "sector", along_sector(0, 1))

    planes = {0: jnp.stack(lines)}
    for e in Z_ORDER:
        planes[e] = lax.ppermute(planes[0], "sector", along_sector(e, 0))
    planes = [planes[e] for e in PLANES]
    planes = planes + [lax.ppermute(p, "sector", along_sector(0, 1)) for p in planes]
    own, wave = choose(meta, own_half(mine), planes)
    parts = far_half(meta, mine, theirs, own, wave, right_blocks)
    return finish(parts[0], [lax.ppermute(parts[d], "table", along_table(d, 0)) for d in (2, 1, 3)])


def solution(mesh):
    placed = (
        P("sector", "table", None),
        P("table", None, None),
        P("sector", None, None),
        P("sector"),
        P("sector", None),
        P("sector", None, None),
        P(("sector", "table")),
        P(("sector", "table")),
        P(("sector", "table")),
        P(("sector", "table")),
    )
    return jax.shard_map(
        local, mesh=mesh, in_specs=placed, out_specs=P("sector", "table", None), check_vma=False
    )
```

```python
import functools

import jax
import jax.numpy as jnp
from jax import lax
from jax.experimental import pallas as pl
from jax.experimental.pallas import tpu as pltpu
from jax.sharding import PartitionSpec as P

BF = jnp.bfloat16
F32 = jnp.float32
SIDE = 4
TABS = 16
ROWS = 16
HALF = 64
WIDTH = 256
SLOTS = 16
PICKS = 24
PAIRS = SLOTS * PICKS
SHARE = ROWS * 128
SENT = SHARE + PAIRS
DEPTH = PICKS * HALF
PITCH = PAIRS + 8
ROW_PITCH = ROWS + 8
PACK_MIB = 16
MIB = 1 << 20
ENV = 4
SIZE = ENV + SLOTS
FETCH = SIZE + SLOTS // 2
LISTED = 3
CHUNK = 256
LIMIT = 32700.0
STEP = SLOTS * ROWS
X_ORDER = (2, 1, 3)
Z_ORDER = (2, 1, 3)
PLANES = (0, 2, 1, 3)
CHOOSE_COST = 1_000_000_000
OWN_COST = 100_000_000_000
FAR_COST = 4_000_000_000
WEIGH_COST = 100_000_000_000


def in_hbm(value):
    return pltpu.with_memory_space_constraint(value, pltpu.HBM)


def swap_halves(value):
    return pltpu.roll(value, 64, 1)


def pack_kernel(meta, blocks, pick_in, tab_in, slot_in, live_in, out_ref, held, lists, rows, ready, sems, list_sems, out_sems):
    core = meta[0]

    def fetch(x, u):
        source = blocks.at[:, core + 2 * u, pl.ds(x * ROWS, ROWS), :]
        return pltpu.make_async_copy(source, held.at[x, u], sems.at[x, u])

    def hand(x):
        return pltpu.make_async_copy(ready.at[x], out_ref.at[:, x], out_sems.at[x])

    for x in range(SIDE):
        for u in range(2):
            fetch(x, u).start()
    copies = []
    for n, ref in enumerate((pick_in, tab_in, slot_in, live_in)):
        copies.append(pltpu.make_async_copy(ref, lists.at[n], list_sems.at[n]))
        copies[n].start()
    def count():
        for copy in copies:
            copy.wait()

        terms = pick_in.shape[1]
        tab_hot = (lax.broadcasted_iota(jnp.int32, (TABS, terms), 0) == lists[1]) & (lists[3] > 0)
        pair = lists[2] * PICKS + lists[0]
        pair_hot = lax.broadcasted_iota(jnp.int32, (PAIRS, terms), 0) == pair
        counts = lax.dot_general(
            tab_hot.astype(F32).astype(BF),
            pair_hot.astype(F32).astype(BF),
            (((1,), (1,)), ((), ())),
            preferred_element_type=F32,
        ).astype(BF)
        return counts

    low = lax.broadcasted_iota(jnp.int32, (TABS, 128), 1) < 64
    for x in range(SIDE):
        for u in range(2):
            fetch(x, u).wait()
            for t in range(TABS):
                block = held[x, u, t].astype(F32)
                for k in range(2):
                    rows[k, u, t * ROW_PITCH : t * ROW_PITCH + ROWS, :] = block[:, k * 128 : k * 128 + 128]
        if x == 0:
            counts = count()
        for y in range(SIDE):
            ready[x, y, :, SHARE:SENT] = counts
        for q in range(ROWS):
            lanes = slice(q * 128, q * 128 + 128)
            for k in range(2):
                a = rows[k, 0, pl.ds(q, TABS, stride=ROW_PITCH), :]
                b = rows[k, 1, pl.ds(q, TABS, stride=ROW_PITCH), :]
                mixed = swap_halves(jnp.where(low, b, a))
                ready[x, 2 * k, :, lanes] = jnp.where(low, a, mixed).astype(BF)
                ready[x, 2 * k + 1, :, lanes] = jnp.where(low, mixed, b).astype(BF)
        hand(x).start()
    for x in range(SIDE):
        hand(x).wait()


def pack(meta, recoupling, pick, tab, slot, live):
    there = pl.BlockSpec(memory_space=pltpu.HBM)
    out = pl.pallas_call(
        pack_kernel,
        in_specs=[pl.BlockSpec(memory_space=pltpu.SMEM)] + [there] * 5,
        out_specs=there,
        out_shape=pltpu.HBM((SIDE, SIDE, TABS, SENT), BF),
        scratch_shapes=[
            pltpu.VMEM((SIDE, 2, TABS, ROWS, WIDTH), BF),
            pltpu.VMEM((4, 1, pick.shape[0]), jnp.int32),
            pltpu.VMEM((2, 2, TABS * ROW_PITCH, 128), F32),
            pltpu.VMEM((SIDE, SIDE, TABS, SENT), BF),
            pltpu.SemaphoreType.DMA((SIDE, 2)),
            pltpu.SemaphoreType.DMA((4,)),
            pltpu.SemaphoreType.DMA((SIDE,)),
        ],
        compiler_params=pltpu.CompilerParams(vmem_limit_bytes=PACK_MIB * MIB),
        name="pack",
    )(
        meta,
        in_hbm(recoupling.reshape(TABS, SIDE, HALF, WIDTH)),
        *(in_hbm(v.reshape(1, -1)) for v in (pick, tab, slot, live)),
    )
    return out.reshape(SIDE * SIDE, TABS, SENT)


def spread(counts_ref, share_ref, sums, hi_ref, lo_ref):
    counts = counts_ref[:, SHARE:SENT]
    for n in range(ROWS // 2):
        part = lax.dot_general(
            counts, share_ref[:, n * 256 : n * 256 + 256], (((0,), (0,)), ((), ())), preferred_element_type=F32
        )
        for k in range(2):
            start = (2 * n + k) * PITCH
            sums[start : start + PAIRS, :] = part[:, k * 128 : k * 128 + 128]
    low = lax.broadcasted_iota(jnp.int32, (ROWS, 128), 1) < 64

    for s in range(SLOTS):
        for k in range(PICKS // 2):
            row = s * PICKS + 2 * k
            a = sums[pl.ds(row, ROWS, stride=PITCH), :]
            b = sums[pl.ds(row + 1, ROWS, stride=PITCH), :]
            mixed = swap_halves(jnp.where(low, b, a))
            for u, value in enumerate((jnp.where(low, a, mixed), jnp.where(low, mixed, b))):
                hi = value.astype(BF)
                place = slice((2 * s + u) * ROWS, (2 * s + u + 1) * ROWS)
                hi_ref[place, k * 128 : k * 128 + 128] = hi
                lo_ref[place, k * 128 : k * 128 + 128] = (value - hi.astype(F32)).astype(BF)


def multiply(hi_ref, lo_ref, weights, n):
    rows = slice(n * CHUNK, (n + 1) * CHUNK)
    part = jnp.dot(hi_ref[rows, :], weights, preferred_element_type=F32)
    return part + jnp.dot(lo_ref[rows, :], weights, preferred_element_type=F32)


def own_kernel(mine, hi_ref, lo_ref, sums):
    spread(mine, mine, sums, hi_ref, lo_ref)


def own_half(mine):
    here = pl.BlockSpec(memory_space=pltpu.VMEM)
    return pl.pallas_call(
        own_kernel,
        in_specs=[here],
        out_specs=[here] * 2,
        out_shape=[pltpu.VMEM((2 * STEP, DEPTH), BF)] * 2,
        scratch_shapes=[pltpu.VMEM((ROWS * PITCH, 128), F32)],
        compiler_params=pltpu.CompilerParams(vmem_limit_bytes=16 * MIB),
        cost_estimate=pl.CostEstimate(flops=OWN_COST, bytes_accessed=MIB, transcendentals=0),
        name="own_half",
    )(mine)


def choose_kernel(meta, hi_ref, lo_ref, *refs):
    planes, (out_ref, wave) = refs[:8], refs[8:]
    core, x, z = meta[0], meta[1], meta[3]
    for c in range(2):
        for place, e in enumerate(PLANES):
            group = 2 * lax.rem(z - e + SIDE, SIDE) + (core if c == 0 else 1 - core)
            for n in range(LISTED):
                pick = LISTED * group + n
                piece = meta[FETCH + pick]
                for d in range(SIDE):
                    rows = pl.ds(pl.multiple_of(lax.rem(x - d + SIDE, SIDE) * ROWS, ROWS), ROWS)
                    wave[pick, rows, :] = planes[c * SIDE + place][d, piece]
    weights = wave[...].reshape(DEPTH, WIDTH)
    for n in range(2 * STEP // CHUNK):
        out_ref[n * CHUNK : (n + 1) * CHUNK, :] = multiply(hi_ref, lo_ref, weights, n)


def choose(meta, own, planes):
    here = pl.BlockSpec(memory_space=pltpu.VMEM)
    return pl.pallas_call(
        choose_kernel,
        in_specs=[pl.BlockSpec(memory_space=pltpu.SMEM)] + [here] * 10,
        out_specs=[here] * 2,
        out_shape=[pltpu.VMEM((2 * STEP, WIDTH), F32), pltpu.VMEM((PICKS, HALF, WIDTH), BF)],
        compiler_params=pltpu.CompilerParams(vmem_limit_bytes=16 * MIB),
        cost_estimate=pl.CostEstimate(flops=CHOOSE_COST, bytes_accessed=MIB, transcendentals=0),
        name="choose",
    )(meta, *own, *planes)


def far_kernel(meta, mine, theirs, own, wave, right, s0, s1, s2, s3, sums, hi_ref, lo_ref, channel, codes):
    core, x, y = meta[0], meta[1], meta[2]
    codes[...] = jnp.zeros_like(codes)
    spread(mine, theirs, sums, hi_ref, lo_ref)
    weights = wave[...].reshape(DEPTH, WIDTH)
    for s in range(SLOTS):
        for u in range(2):
            step = lax.rem(2 * u + core - y + SIDE, SIDE)
            channel[step, s * ROWS : (s + 1) * ROWS, :] = own[(2 * s + u) * ROWS : (2 * s + u + 1) * ROWS, :]
    for n in range(2 * STEP // CHUNK):
        part = multiply(hi_ref, lo_ref, weights, n)
        for m in range(CHUNK // ROWS):
            s, u = divmod(n * (CHUNK // ROWS) + m, 2)
            step = lax.rem(2 * u + 1 - core - y + SIDE, SIDE)
            channel[step, s * ROWS : (s + 1) * ROWS, :] = part[m * ROWS : (m + 1) * ROWS]
    columns = lax.broadcasted_iota(jnp.int32, (ROWS, WIDTH), 1)
    lines = lax.broadcasted_iota(jnp.int32, (ROWS, WIDTH), 0)
    reach = [jnp.maximum(lines + (lax.rem(y + d, SIDE) * SIDE + x) * ROWS, columns) for d in range(SIDE)]
    for o in range(SLOTS // 2):
        hi, lo, env = [], [], []
        for s in (2 * o, 2 * o + 1):
            env.append(right[meta[ENV + s]])
            value = channel[:, s * ROWS : (s + 1) * ROWS, :].reshape(HALF, WIDTH)
            hi.append(value.astype(BF))
            lo.append((value - hi[-1].astype(F32)).astype(BF))
        both = jnp.concatenate([jnp.concatenate(hi, axis=1), jnp.concatenate(lo, axis=1)], axis=0)
        result = jnp.dot(both, jnp.concatenate(env, axis=0), preferred_element_type=F32)
        result = result[:HALF] + result[HALF:]
        size = meta[SIZE + o]
        for d, ref in enumerate((s0, s1, s2, s3)):
            part = jnp.where(reach[d] < size, result[d * ROWS : (d + 1) * ROWS], 0.0)
            if d == 0:
                ref[o] = part
                continue
            peak = jnp.max(jnp.abs(part), axis=0, keepdims=True)
            code = jnp.ceil(jnp.log2(jnp.maximum(peak, 1e-30)) * 8.0 + 0.01)
            scaled = part * (jnp.exp2(code * -0.125) * LIMIT)
            ref[o] = jnp.round(scaled).astype(jnp.int32).astype(jnp.int16)
            codes[d - 1, o : o + 1, :] = code
    for d, ref in enumerate((s1, s2, s3)):
        ref[SLOTS // 2] = codes[d].astype(jnp.int32).astype(jnp.int16)


def far_half(meta, mine, theirs, own, wave, right):
    sectors = SLOTS // 2
    here = pl.BlockSpec(memory_space=pltpu.VMEM)
    return pl.pallas_call(
        far_kernel,
        in_specs=[pl.BlockSpec(memory_space=pltpu.SMEM)] + [here] * 5,
        out_specs=[here] * 4,
        out_shape=[pltpu.VMEM((sectors, ROWS, WIDTH), F32)] + [pltpu.VMEM((sectors + 1, ROWS, WIDTH), jnp.int16)] * 3,
        scratch_shapes=[
            pltpu.VMEM((ROWS * PITCH, 128), F32),
            pltpu.VMEM((2 * STEP, DEPTH), BF),
            pltpu.VMEM((2 * STEP, DEPTH), BF),
            pltpu.VMEM((SIDE, STEP, WIDTH), F32),
            pltpu.VMEM((3, ROWS, WIDTH), F32),
        ],
        compiler_params=pltpu.CompilerParams(vmem_limit_bytes=24 * MIB),
        cost_estimate=pl.CostEstimate(flops=FAR_COST, bytes_accessed=MIB, transcendentals=0),
        name="far_half",
    )(meta, mine, theirs, own, wave, right)


def finish_kernel(own, *refs):
    parts, out_ref = refs[:-1], refs[-1]
    scales = [jnp.exp2(ref[SLOTS // 2].astype(jnp.int32).astype(F32) * 0.125) * (1.0 / LIMIT) for ref in parts]
    for o in range(SLOTS // 2):
        total = own[o]
        for ref, scale in zip(parts, scales):
            total = total + ref[o].astype(jnp.int32).astype(F32) * scale[o : o + 1]
        out_ref[o] = total


def finish(own, parts):
    here = pl.BlockSpec(memory_space=pltpu.VMEM)
    return pl.pallas_call(
        finish_kernel,
        in_specs=[here] * 4,
        out_specs=here,
        out_shape=jax.ShapeDtypeStruct(own.shape, F32),
        compiler_params=pltpu.CompilerParams(vmem_limit_bytes=4 * MIB),
        name="finish",
    )(own, *parts)


def along_table(dy, dx):
    return [
        (y * SIDE + x, (y + dy) % SIDE * SIDE + (x + dx) % SIDE) for y in range(SIDE) for x in range(SIDE)
    ]


def along_sector(dz, dc):
    return [(z * 2 + c, (z + dz) % SIDE * 2 + (c ^ dc)) for z in range(SIDE) for c in range(2)]


def local(
    wave_blocks,
    recoupling,
    right_blocks,
    sector_sizes,
    channel_env,
    fetch_list,
    term_pick,
    term_table,
    term_slot,
    term_live,
):
    sector = lax.axis_index("sector")
    place = lax.axis_index("table")
    z, core = sector // 2, sector % 2
    y, x = place // SIDE, place % SIDE

    meta = jnp.concatenate(
        [jnp.stack([core, x, y, z]), channel_env.reshape(-1), sector_sizes, fetch_list.reshape(-1)]
    )

    lines = {0: wave_blocks}
    for d in X_ORDER:
        lines[d] = lax.ppermute(wave_blocks, "table", along_table(0, d))
    lines = [lines[d] for d in range(SIDE)]
    sent = pack(core.reshape(1), recoupling, term_pick, term_table, term_slot, term_live)
    sent, lines = lax.optimization_barrier((sent, lines))
    mine = lax.all_to_all(sent, "table", 0, 0).reshape(TABS * SIDE * SIDE, SENT)
    theirs = lax.ppermute(mine, "sector", along_sector(0, 1))

    planes = {0: jnp.stack(lines)}
    for e in Z_ORDER:
        planes[e] = lax.ppermute(planes[0], "sector", along_sector(e, 0))
    planes = [planes[e] for e in PLANES]
    planes = planes + [lax.ppermute(p, "sector", along_sector(0, 1)) for p in planes]
    own, wave = choose(meta, own_half(mine), planes)
    parts = far_half(meta, mine, theirs, own, wave, right_blocks)
    return finish(parts[0], [lax.ppermute(parts[d], "table", along_table(d, 0)) for d in (2, 1, 3)])


def solution(mesh):
    placed = (
        P("sector", "table", None),
        P("table", None, None),
        P("sector", None, None),
        P("sector"),
        P("sector", None),
        P("sector", None, None),
        P(("sector", "table")),
        P(("sector", "table")),
        P(("sector", "table")),
        P(("sector", "table")),
    )
    return jax.shard_map(
        local, mesh=mesh, in_specs=placed, out_specs=P("sector", "table", None), check_vma=False
    )
```

```python
import functools

import jax
import jax.numpy as jnp
from jax import lax
from jax.experimental import pallas as pl
from jax.experimental.pallas import tpu as pltpu
from jax.sharding import PartitionSpec as P

BF = jnp.bfloat16
F32 = jnp.float32
SIDE = 4
TABS = 16
ROWS = 16
HALF = 64
WIDTH = 256
SLOTS = 16
PICKS = 24
PAIRS = SLOTS * PICKS
SHARE = ROWS * 128
SENT = SHARE + PAIRS
DEPTH = PICKS * HALF
PITCH = PAIRS + 8
ROW_PITCH = ROWS + 8
PACK_MIB = 16
MIB = 1 << 20
ENV = 4
SIZE = ENV + SLOTS
FETCH = SIZE + SLOTS // 2
LISTED = 3
CHUNK = 128
LIMIT = 32700.0
STEP = SLOTS * ROWS
X_ORDER = (2, 1, 3)
Z_ORDER = (2, 1, 3)
PLANES = (0, 2, 1, 3)
CHOOSE_COST = 1_000_000_000
OWN_COST = 100_000_000_000
FAR_COST = 4_000_000_000
WEIGH_COST = 100_000_000_000


def in_hbm(value):
    return pltpu.with_memory_space_constraint(value, pltpu.HBM)


def swap_halves(value):
    return pltpu.roll(value, 64, 1)


def pack_kernel(meta, blocks, pick_in, tab_in, slot_in, live_in, out_ref, held, lists, rows, ready, sems, list_sems, out_sems):
    core = meta[0]

    def fetch(x, u):
        source = blocks.at[:, core + 2 * u, pl.ds(x * ROWS, ROWS), :]
        return pltpu.make_async_copy(source, held.at[x, u], sems.at[x, u])

    def hand(x):
        return pltpu.make_async_copy(ready.at[x], out_ref.at[:, x], out_sems.at[x])

    for x in range(SIDE):
        for u in range(2):
            fetch(x, u).start()
    copies = []
    for n, ref in enumerate((pick_in, tab_in, slot_in, live_in)):
        copies.append(pltpu.make_async_copy(ref, lists.at[n], list_sems.at[n]))
        copies[n].start()
    def count():
        for copy in copies:
            copy.wait()

        terms = pick_in.shape[1]
        tab_hot = (lax.broadcasted_iota(jnp.int32, (TABS, terms), 0) == lists[1]) & (lists[3] > 0)
        pair = lists[2] * PICKS + lists[0]
        pair_hot = lax.broadcasted_iota(jnp.int32, (PAIRS, terms), 0) == pair
        counts = lax.dot_general(
            tab_hot.astype(F32).astype(BF),
            pair_hot.astype(F32).astype(BF),
            (((1,), (1,)), ((), ())),
            preferred_element_type=F32,
        ).astype(BF)
        return counts

    low = lax.broadcasted_iota(jnp.int32, (TABS, 128), 1) < 64
    for x in range(SIDE):
        for u in range(2):
            fetch(x, u).wait()
            for t in range(TABS):
                block = held[x, u, t].astype(F32)
                for k in range(2):
                    rows[k, u, t * ROW_PITCH : t * ROW_PITCH + ROWS, :] = block[:, k * 128 : k * 128 + 128]
        if x == 0:
            counts = count()
        for y in range(SIDE):
            ready[x, y, :, SHARE:SENT] = counts
        for q in range(ROWS):
            lanes = slice(q * 128, q * 128 + 128)
            for k in range(2):
                a = rows[k, 0, pl.ds(q, TABS, stride=ROW_PITCH), :]
                b = rows[k, 1, pl.ds(q, TABS, stride=ROW_PITCH), :]
                mixed = swap_halves(jnp.where(low, b, a))
                ready[x, 2 * k, :, lanes] = jnp.where(low, a, mixed).astype(BF)
                ready[x, 2 * k + 1, :, lanes] = jnp.where(low, mixed, b).astype(BF)
        hand(x).start()
    for x in range(SIDE):
        hand(x).wait()


def pack(meta, recoupling, pick, tab, slot, live):
    there = pl.BlockSpec(memory_space=pltpu.HBM)
    out = pl.pallas_call(
        pack_kernel,
        in_specs=[pl.BlockSpec(memory_space=pltpu.SMEM)] + [there] * 5,
        out_specs=there,
        out_shape=pltpu.HBM((SIDE, SIDE, TABS, SENT), BF),
        scratch_shapes=[
            pltpu.VMEM((SIDE, 2, TABS, ROWS, WIDTH), BF),
            pltpu.VMEM((4, 1, pick.shape[0]), jnp.int32),
            pltpu.VMEM((2, 2, TABS * ROW_PITCH, 128), F32),
            pltpu.VMEM((SIDE, SIDE, TABS, SENT), BF),
            pltpu.SemaphoreType.DMA((SIDE, 2)),
            pltpu.SemaphoreType.DMA((4,)),
            pltpu.SemaphoreType.DMA((SIDE,)),
        ],
        compiler_params=pltpu.CompilerParams(vmem_limit_bytes=PACK_MIB * MIB),
        name="pack",
    )(
        meta,
        in_hbm(recoupling.reshape(TABS, SIDE, HALF, WIDTH)),
        *(in_hbm(v.reshape(1, -1)) for v in (pick, tab, slot, live)),
    )
    return out.reshape(SIDE * SIDE, TABS, SENT)


def spread(counts_ref, share_ref, sums, hi_ref, lo_ref):
    counts = counts_ref[:, SHARE:SENT]
    for n in range(ROWS // 2):
        part = lax.dot_general(
            counts, share_ref[:, n * 256 : n * 256 + 256], (((0,), (0,)), ((), ())), preferred_element_type=F32
        )
        for k in range(2):
            start = (2 * n + k) * PITCH
            sums[start : start + PAIRS, :] = part[:, k * 128 : k * 128 + 128]
    low = lax.broadcasted_iota(jnp.int32, (ROWS, 128), 1) < 64

    for s in range(SLOTS):
        for k in range(PICKS // 2):
            row = s * PICKS + 2 * k
            a = sums[pl.ds(row, ROWS, stride=PITCH), :]
            b = sums[pl.ds(row + 1, ROWS, stride=PITCH), :]
            mixed = swap_halves(jnp.where(low, b, a))
            for u, value in enumerate((jnp.where(low, a, mixed), jnp.where(low, mixed, b))):
                hi = value.astype(BF)
                place = slice((2 * s + u) * ROWS, (2 * s + u + 1) * ROWS)
                hi_ref[place, k * 128 : k * 128 + 128] = hi
                lo_ref[place, k * 128 : k * 128 + 128] = (value - hi.astype(F32)).astype(BF)


def multiply(hi_ref, lo_ref, weights, n):
    rows = slice(n * CHUNK, (n + 1) * CHUNK)
    part = jnp.dot(hi_ref[rows, :], weights, preferred_element_type=F32)
    return part + jnp.dot(lo_ref[rows, :], weights, preferred_element_type=F32)


def own_kernel(mine, hi_ref, lo_ref, sums):
    spread(mine, mine, sums, hi_ref, lo_ref)


def own_half(mine):
    here = pl.BlockSpec(memory_space=pltpu.VMEM)
    return pl.pallas_call(
        own_kernel,
        in_specs=[here],
        out_specs=[here] * 2,
        out_shape=[pltpu.VMEM((2 * STEP, DEPTH), BF)] * 2,
        scratch_shapes=[pltpu.VMEM((ROWS * PITCH, 128), F32)],
        compiler_params=pltpu.CompilerParams(vmem_limit_bytes=16 * MIB),
        cost_estimate=pl.CostEstimate(flops=OWN_COST, bytes_accessed=MIB, transcendentals=0),
        name="own_half",
    )(mine)


def choose_kernel(meta, hi_ref, lo_ref, *refs):
    planes, (out_ref, wave) = refs[:8], refs[8:]
    core, x, z = meta[0], meta[1], meta[3]
    for c in range(2):
        for place, e in enumerate(PLANES):
            group = 2 * lax.rem(z - e + SIDE, SIDE) + (core if c == 0 else 1 - core)
            for n in range(LISTED):
                pick = LISTED * group + n
                piece = meta[FETCH + pick]
                for d in range(SIDE):
                    rows = pl.ds(pl.multiple_of(lax.rem(x - d + SIDE, SIDE) * ROWS, ROWS), ROWS)
                    wave[pick, rows, :] = planes[c * SIDE + place][d, piece]
    weights = wave[...].reshape(DEPTH, WIDTH)
    for n in range(2 * STEP // CHUNK):
        out_ref[n * CHUNK : (n + 1) * CHUNK, :] = multiply(hi_ref, lo_ref, weights, n)


def choose(meta, own, planes):
    here = pl.BlockSpec(memory_space=pltpu.VMEM)
    return pl.pallas_call(
        choose_kernel,
        in_specs=[pl.BlockSpec(memory_space=pltpu.SMEM)] + [here] * 10,
        out_specs=[here] * 2,
        out_shape=[pltpu.VMEM((2 * STEP, WIDTH), F32), pltpu.VMEM((PICKS, HALF, WIDTH), BF)],
        compiler_params=pltpu.CompilerParams(vmem_limit_bytes=16 * MIB),
        cost_estimate=pl.CostEstimate(flops=CHOOSE_COST, bytes_accessed=MIB, transcendentals=0),
        name="choose",
    )(meta, *own, *planes)


def far_kernel(table, mine, theirs, own, wave, right, s0, s1, s2, s3, sums, hi_ref, lo_ref, channel, codes, meta, meta_sem):
    fetch = pltpu.make_async_copy(table, meta, meta_sem)
    fetch.start()
    codes[...] = jnp.zeros_like(codes)
    spread(mine, theirs, sums, hi_ref, lo_ref)
    fetch.wait()
    core, x, y = meta[0], meta[1], meta[2]
    weights = wave[...].reshape(DEPTH, WIDTH)
    for s in range(SLOTS):
        for u in range(2):
            step = lax.rem(2 * u + core - y + SIDE, SIDE)
            channel[step, s * ROWS : (s + 1) * ROWS, :] = own[(2 * s + u) * ROWS : (2 * s + u + 1) * ROWS, :]
    for n in range(2 * STEP // CHUNK):
        part = multiply(hi_ref, lo_ref, weights, n)
        for m in range(CHUNK // ROWS):
            s, u = divmod(n * (CHUNK // ROWS) + m, 2)
            step = lax.rem(2 * u + 1 - core - y + SIDE, SIDE)
            channel[step, s * ROWS : (s + 1) * ROWS, :] = part[m * ROWS : (m + 1) * ROWS]
    columns = lax.broadcasted_iota(jnp.int32, (ROWS, WIDTH), 1)
    lines = lax.broadcasted_iota(jnp.int32, (ROWS, WIDTH), 0)
    reach = [jnp.maximum(lines + (lax.rem(y + d, SIDE) * SIDE + x) * ROWS, columns) for d in range(SIDE)]
    for o in range(SLOTS // 2):
        hi, lo, env = [], [], []
        for s in (2 * o, 2 * o + 1):
            env.append(right[meta[ENV + s]])
            value = channel[:, s * ROWS : (s + 1) * ROWS, :].reshape(HALF, WIDTH)
            hi.append(value.astype(BF))
            lo.append((value - hi[-1].astype(F32)).astype(BF))
        both = jnp.concatenate([jnp.concatenate(hi, axis=1), jnp.concatenate(lo, axis=1)], axis=0)
        result = jnp.dot(both, jnp.concatenate(env, axis=0), preferred_element_type=F32)
        result = result[:HALF] + result[HALF:]
        size = meta[SIZE + o]
        for d, ref in enumerate((s0, s1, s2, s3)):
            part = jnp.where(reach[d] < size, result[d * ROWS : (d + 1) * ROWS], 0.0)
            if d == 0:
                ref[o] = part
                continue
            peak = jnp.max(jnp.abs(part), axis=0, keepdims=True)
            code = jnp.ceil(jnp.log2(jnp.maximum(peak, 1e-30)) * 8.0 + 0.01)
            scaled = part * (jnp.exp2(code * -0.125) * LIMIT)
            ref[o] = jnp.round(scaled).astype(jnp.int32).astype(jnp.int16)
            codes[d - 1, o : o + 1, :] = code
    for d, ref in enumerate((s1, s2, s3)):
        ref[SLOTS // 2] = codes[d].astype(jnp.int32).astype(jnp.int16)


def far_half(meta, mine, theirs, own, wave, right):
    sectors = SLOTS // 2
    here = pl.BlockSpec(memory_space=pltpu.VMEM)
    return pl.pallas_call(
        far_kernel,
        in_specs=[pl.BlockSpec(memory_space=pl.ANY)] + [here] * 5,
        out_specs=[here] * 4,
        out_shape=[pltpu.VMEM((sectors, ROWS, WIDTH), F32)] + [pltpu.VMEM((sectors + 1, ROWS, WIDTH), jnp.int16)] * 3,
        scratch_shapes=[
            pltpu.VMEM((ROWS * PITCH, 128), F32),
            pltpu.VMEM((2 * STEP, DEPTH), BF),
            pltpu.VMEM((2 * STEP, DEPTH), BF),
            pltpu.VMEM((SIDE, STEP, WIDTH), F32),
            pltpu.VMEM((3, ROWS, WIDTH), F32),
            pltpu.SMEM(meta.shape, jnp.int32),
            pltpu.SemaphoreType.DMA(()),
        ],
        compiler_params=pltpu.CompilerParams(vmem_limit_bytes=24 * MIB),
        cost_estimate=pl.CostEstimate(flops=FAR_COST, bytes_accessed=MIB, transcendentals=0),
        name="far_half",
    )(meta, mine, theirs, own, wave, right)


def finish_kernel(own, *refs):
    parts, out_ref = refs[:-1], refs[-1]
    scales = [jnp.exp2(ref[SLOTS // 2].astype(jnp.int32).astype(F32) * 0.125) * (1.0 / LIMIT) for ref in parts]
    for o in range(SLOTS // 2):
        total = own[o]
        for ref, scale in zip(parts, scales):
            total = total + ref[o].astype(jnp.int32).astype(F32) * scale[o : o + 1]
        out_ref[o] = total


def finish(own, parts):
    here = pl.BlockSpec(memory_space=pltpu.VMEM)
    return pl.pallas_call(
        finish_kernel,
        in_specs=[here] * 4,
        out_specs=here,
        out_shape=jax.ShapeDtypeStruct(own.shape, F32),
        compiler_params=pltpu.CompilerParams(vmem_limit_bytes=4 * MIB),
        name="finish",
    )(own, *parts)


def along_table(dy, dx):
    return [
        (y * SIDE + x, (y + dy) % SIDE * SIDE + (x + dx) % SIDE) for y in range(SIDE) for x in range(SIDE)
    ]


def along_sector(dz, dc):
    return [(z * 2 + c, (z + dz) % SIDE * 2 + (c ^ dc)) for z in range(SIDE) for c in range(2)]


def local(
    wave_blocks,
    recoupling,
    right_blocks,
    sector_sizes,
    channel_env,
    fetch_list,
    term_pick,
    term_table,
    term_slot,
    term_live,
):
    sector = lax.axis_index("sector")
    place = lax.axis_index("table")
    z, core = sector // 2, sector % 2
    y, x = place // SIDE, place % SIDE

    meta = jnp.concatenate(
        [jnp.stack([core, x, y, z]), channel_env.reshape(-1), sector_sizes, fetch_list.reshape(-1)]
    )

    lines = {0: wave_blocks}
    for d in X_ORDER:
        lines[d] = lax.ppermute(wave_blocks, "table", along_table(0, d))
    lines = [lines[d] for d in range(SIDE)]
    sent = pack(core.reshape(1), recoupling, term_pick, term_table, term_slot, term_live)
    sent, lines = lax.optimization_barrier((sent, lines))
    mine = lax.all_to_all(sent, "table", 0, 0).reshape(TABS * SIDE * SIDE, SENT)
    theirs = lax.ppermute(mine, "sector", along_sector(0, 1))

    planes = {0: jnp.stack(lines)}
    for e in Z_ORDER:
        planes[e] = lax.ppermute(planes[0], "sector", along_sector(e, 0))
    planes = [planes[e] for e in PLANES]
    planes = planes + [lax.ppermute(p, "sector", along_sector(0, 1)) for p in planes]
    own, wave = choose(meta, own_half(mine), planes)
    parts = far_half(meta, mine, theirs, own, wave, right_blocks)
    return finish(parts[0], [lax.ppermute(parts[d], "table", along_table(d, 0)) for d in (2, 1, 3)])


def solution(mesh):
    placed = (
        P("sector", "table", None),
        P("table", None, None),
        P("sector", None, None),
        P("sector"),
        P("sector", None),
        P("sector", None, None),
        P(("sector", "table")),
        P(("sector", "table")),
        P(("sector", "table")),
        P(("sector", "table")),
    )
    return jax.shard_map(
        local, mesh=mesh, in_specs=placed, out_specs=P("sector", "table", None), check_vma=False
    )
```

```python
import functools

import jax
import jax.numpy as jnp
from jax import lax
from jax.experimental import pallas as pl
from jax.experimental.pallas import tpu as pltpu
from jax.sharding import PartitionSpec as P

BF = jnp.bfloat16
F32 = jnp.float32
SIDE = 4
TABS = 16
ROWS = 16
HALF = 64
WIDTH = 256
SLOTS = 16
PICKS = 24
PAIRS = SLOTS * PICKS
SHARE = ROWS * 128
SENT = SHARE + PAIRS
DEPTH = PICKS * HALF
PITCH = PAIRS + 8
ROW_PITCH = ROWS + 8
PACK_MIB = 16
MIB = 1 << 20
ENV = 4
SIZE = ENV + SLOTS
FETCH = SIZE + SLOTS // 2
LISTED = 3
CHUNK = 128
LIMIT = 32700.0
STEP = SLOTS * ROWS
X_ORDER = (2, 1, 3)
Z_ORDER = (2, 1, 3)
PLANES = (0, 2, 1, 3)
CHOOSE_COST = 1_000_000_000
OWN_COST = 100_000_000_000
FAR_COST = 4_000_000_000
WEIGH_COST = 100_000_000_000


def in_hbm(value):
    return pltpu.with_memory_space_constraint(value, pltpu.HBM)


def swap_halves(value):
    return pltpu.roll(value, 64, 1)


def pack_kernel(meta, blocks, pick_in, tab_in, slot_in, live_in, out_ref, held, lists, rows, ready, sems, list_sems, out_sems):
    core = meta[0]

    def fetch(x, u):
        source = blocks.at[:, core + 2 * u, pl.ds(x * ROWS, ROWS), :]
        return pltpu.make_async_copy(source, held.at[x, u], sems.at[x, u])

    def hand(x):
        return pltpu.make_async_copy(ready.at[x], out_ref.at[:, x], out_sems.at[x])

    for x in range(SIDE):
        for u in range(2):
            fetch(x, u).start()
    copies = []
    for n, ref in enumerate((pick_in, tab_in, slot_in, live_in)):
        copies.append(pltpu.make_async_copy(ref, lists.at[n], list_sems.at[n]))
        copies[n].start()
    def count():
        for copy in copies:
            copy.wait()

        terms = pick_in.shape[1]
        tab_hot = (lax.broadcasted_iota(jnp.int32, (TABS, terms), 0) == lists[1]) & (lists[3] > 0)
        pair = lists[2] * PICKS + lists[0]
        pair_hot = lax.broadcasted_iota(jnp.int32, (PAIRS, terms), 0) == pair
        counts = lax.dot_general(
            tab_hot.astype(F32).astype(BF),
            pair_hot.astype(F32).astype(BF),
            (((1,), (1,)), ((), ())),
            preferred_element_type=F32,
        ).astype(BF)
        return counts

    low = lax.broadcasted_iota(jnp.int32, (TABS, 128), 1) < 64
    for x in range(SIDE):
        for u in range(2):
            fetch(x, u).wait()
            for t in range(TABS):
                block = held[x, u, t].astype(F32)
                for k in range(2):
                    rows[k, u, t * ROW_PITCH : t * ROW_PITCH + ROWS, :] = block[:, k * 128 : k * 128 + 128]
        if x == 0:
            counts = count()
        for y in range(SIDE):
            ready[x, y, :, SHARE:SENT] = counts
        for q in range(ROWS):
            lanes = slice(q * 128, q * 128 + 128)
            for k in range(2):
                a = rows[k, 0, pl.ds(q, TABS, stride=ROW_PITCH), :]
                b = rows[k, 1, pl.ds(q, TABS, stride=ROW_PITCH), :]
                mixed = swap_halves(jnp.where(low, b, a))
                ready[x, 2 * k, :, lanes] = jnp.where(low, a, mixed).astype(BF)
                ready[x, 2 * k + 1, :, lanes] = jnp.where(low, mixed, b).astype(BF)
        hand(x).start()
    for x in range(SIDE):
        hand(x).wait()


def pack(meta, recoupling, pick, tab, slot, live):
    there = pl.BlockSpec(memory_space=pltpu.HBM)
    out = pl.pallas_call(
        pack_kernel,
        in_specs=[pl.BlockSpec(memory_space=pltpu.SMEM)] + [there] * 5,
        out_specs=there,
        out_shape=pltpu.HBM((SIDE, SIDE, TABS, SENT), BF),
        scratch_shapes=[
            pltpu.VMEM((SIDE, 2, TABS, ROWS, WIDTH), BF),
            pltpu.VMEM((4, 1, pick.shape[0]), jnp.int32),
            pltpu.VMEM((2, 2, TABS * ROW_PITCH, 128), F32),
            pltpu.VMEM((SIDE, SIDE, TABS, SENT), BF),
            pltpu.SemaphoreType.DMA((SIDE, 2)),
            pltpu.SemaphoreType.DMA((4,)),
            pltpu.SemaphoreType.DMA((SIDE,)),
        ],
        compiler_params=pltpu.CompilerParams(vmem_limit_bytes=PACK_MIB * MIB),
        name="pack",
    )(
        meta,
        in_hbm(recoupling.reshape(TABS, SIDE, HALF, WIDTH)),
        *(in_hbm(v.reshape(1, -1)) for v in (pick, tab, slot, live)),
    )
    return out.reshape(SIDE * SIDE, TABS, SENT)


def weigh(counts_ref, share_ref, sums):
    counts = counts_ref[:, SHARE:SENT]
    for n in range(ROWS // 2):
        part = lax.dot_general(
            counts, share_ref[:, n * 256 : n * 256 + 256], (((0,), (0,)), ((), ())), preferred_element_type=F32
        )
        for k in range(2):
            start = (2 * n + k) * PITCH
            sums[start : start + PAIRS, :] = part[:, k * 128 : k * 128 + 128]


def relay(sums, hi_ref, lo_ref):
    low = lax.broadcasted_iota(jnp.int32, (ROWS, 128), 1) < 64

    for s in range(SLOTS):
        for k in range(PICKS // 2):
            row = s * PICKS + 2 * k
            a = sums[pl.ds(row, ROWS, stride=PITCH), :]
            b = sums[pl.ds(row + 1, ROWS, stride=PITCH), :]
            mixed = swap_halves(jnp.where(low, b, a))
            for u, value in enumerate((jnp.where(low, a, mixed), jnp.where(low, mixed, b))):
                hi = value.astype(BF)
                place = slice((2 * s + u) * ROWS, (2 * s + u + 1) * ROWS)
                hi_ref[place, k * 128 : k * 128 + 128] = hi
                lo_ref[place, k * 128 : k * 128 + 128] = (value - hi.astype(F32)).astype(BF)


def multiply(hi_ref, lo_ref, weights, n):
    rows = slice(n * CHUNK, (n + 1) * CHUNK)
    part = jnp.dot(hi_ref[rows, :], weights, preferred_element_type=F32)
    return part + jnp.dot(lo_ref[rows, :], weights, preferred_element_type=F32)


def own_kernel(mine, sums):
    weigh(mine, mine, sums)


def own_half(mine):
    here = pl.BlockSpec(memory_space=pltpu.VMEM)
    return pl.pallas_call(
        own_kernel,
        in_specs=[here],
        out_specs=here,
        out_shape=pltpu.VMEM((ROWS * PITCH, 128), F32),
        compiler_params=pltpu.CompilerParams(vmem_limit_bytes=16 * MIB),
        cost_estimate=pl.CostEstimate(flops=OWN_COST, bytes_accessed=MIB, transcendentals=0),
        name="own_half",
    )(mine)


def choose_kernel(table, sums, *refs):
    planes, (out_ref, wave, hi_ref, lo_ref, meta, meta_sem) = refs[:8], refs[8:]
    fetch = pltpu.make_async_copy(table, meta, meta_sem)
    fetch.start()
    relay(sums, hi_ref, lo_ref)
    fetch.wait()
    core, x, z = meta[0], meta[1], meta[3]
    for c in range(2):
        for place, e in enumerate(PLANES):
            group = 2 * lax.rem(z - e + SIDE, SIDE) + (core if c == 0 else 1 - core)
            for n in range(LISTED):
                pick = LISTED * group + n
                piece = meta[FETCH + pick]
                for d in range(SIDE):
                    rows = pl.ds(pl.multiple_of(lax.rem(x - d + SIDE, SIDE) * ROWS, ROWS), ROWS)
                    wave[pick, rows, :] = planes[c * SIDE + place][d, piece]
    weights = wave[...].reshape(DEPTH, WIDTH)
    for n in range(2 * STEP // CHUNK):
        out_ref[n * CHUNK : (n + 1) * CHUNK, :] = multiply(hi_ref, lo_ref, weights, n)


def choose(meta, own, planes):
    here = pl.BlockSpec(memory_space=pltpu.VMEM)
    return pl.pallas_call(
        choose_kernel,
        in_specs=[pl.BlockSpec(memory_space=pl.ANY)] + [here] * 9,
        out_specs=[here] * 2,
        out_shape=[pltpu.VMEM((2 * STEP, WIDTH), F32), pltpu.VMEM((PICKS, HALF, WIDTH), BF)],
        scratch_shapes=[
            pltpu.VMEM((2 * STEP, DEPTH), BF),
            pltpu.VMEM((2 * STEP, DEPTH), BF),
            pltpu.SMEM(meta.shape, jnp.int32),
            pltpu.SemaphoreType.DMA(()),
        ],
        compiler_params=pltpu.CompilerParams(vmem_limit_bytes=16 * MIB),
        cost_estimate=pl.CostEstimate(flops=CHOOSE_COST, bytes_accessed=MIB, transcendentals=0),
        name="choose",
    )(meta, own, *planes)


def far_kernel(table, mine, theirs, own, wave, right, s0, s1, s2, s3, sums, hi_ref, lo_ref, channel, codes, meta, meta_sem):
    fetch = pltpu.make_async_copy(table, meta, meta_sem)
    fetch.start()
    codes[...] = jnp.zeros_like(codes)
    weigh(mine, theirs, sums)
    relay(sums, hi_ref, lo_ref)
    fetch.wait()
    core, x, y = meta[0], meta[1], meta[2]
    weights = wave[...].reshape(DEPTH, WIDTH)
    for s in range(SLOTS):
        for u in range(2):
            step = lax.rem(2 * u + core - y + SIDE, SIDE)
            channel[step, s * ROWS : (s + 1) * ROWS, :] = own[(2 * s + u) * ROWS : (2 * s + u + 1) * ROWS, :]
    for n in range(2 * STEP // CHUNK):
        part = multiply(hi_ref, lo_ref, weights, n)
        for m in range(CHUNK // ROWS):
            s, u = divmod(n * (CHUNK // ROWS) + m, 2)
            step = lax.rem(2 * u + 1 - core - y + SIDE, SIDE)
            channel[step, s * ROWS : (s + 1) * ROWS, :] = part[m * ROWS : (m + 1) * ROWS]
    columns = lax.broadcasted_iota(jnp.int32, (ROWS, WIDTH), 1)
    lines = lax.broadcasted_iota(jnp.int32, (ROWS, WIDTH), 0)
    reach = [jnp.maximum(lines + (lax.rem(y + d, SIDE) * SIDE + x) * ROWS, columns) for d in range(SIDE)]
    for o in range(SLOTS // 2):
        hi, lo, env = [], [], []
        for s in (2 * o, 2 * o + 1):
            env.append(right[meta[ENV + s]])
            value = channel[:, s * ROWS : (s + 1) * ROWS, :].reshape(HALF, WIDTH)
            hi.append(value.astype(BF))
            lo.append((value - hi[-1].astype(F32)).astype(BF))
        both = jnp.concatenate([jnp.concatenate(hi, axis=1), jnp.concatenate(lo, axis=1)], axis=0)
        result = jnp.dot(both, jnp.concatenate(env, axis=0), preferred_element_type=F32)
        result = result[:HALF] + result[HALF:]
        size = meta[SIZE + o]
        for d, ref in enumerate((s0, s1, s2, s3)):
            part = jnp.where(reach[d] < size, result[d * ROWS : (d + 1) * ROWS], 0.0)
            if d == 0:
                ref[o] = part
                continue
            peak = jnp.max(jnp.abs(part), axis=0, keepdims=True)
            code = jnp.ceil(jnp.log2(jnp.maximum(peak, 1e-30)) * 8.0 + 0.01)
            scaled = part * (jnp.exp2(code * -0.125) * LIMIT)
            ref[o] = jnp.round(scaled).astype(jnp.int32).astype(jnp.int16)
            codes[d - 1, o : o + 1, :] = code
    for d, ref in enumerate((s1, s2, s3)):
        ref[SLOTS // 2] = codes[d].astype(jnp.int32).astype(jnp.int16)


def far_half(meta, mine, theirs, own, wave, right):
    sectors = SLOTS // 2
    here = pl.BlockSpec(memory_space=pltpu.VMEM)
    return pl.pallas_call(
        far_kernel,
        in_specs=[pl.BlockSpec(memory_space=pl.ANY)] + [here] * 5,
        out_specs=[here] * 4,
        out_shape=[pltpu.VMEM((sectors, ROWS, WIDTH), F32)] + [pltpu.VMEM((sectors + 1, ROWS, WIDTH), jnp.int16)] * 3,
        scratch_shapes=[
            pltpu.VMEM((ROWS * PITCH, 128), F32),
            pltpu.VMEM((2 * STEP, DEPTH), BF),
            pltpu.VMEM((2 * STEP, DEPTH), BF),
            pltpu.VMEM((SIDE, STEP, WIDTH), F32),
            pltpu.VMEM((3, ROWS, WIDTH), F32),
            pltpu.SMEM(meta.shape, jnp.int32),
            pltpu.SemaphoreType.DMA(()),
        ],
        compiler_params=pltpu.CompilerParams(vmem_limit_bytes=24 * MIB),
        cost_estimate=pl.CostEstimate(flops=FAR_COST, bytes_accessed=MIB, transcendentals=0),
        name="far_half",
    )(meta, mine, theirs, own, wave, right)


def finish_kernel(own, *refs):
    parts, out_ref = refs[:-1], refs[-1]
    scales = [jnp.exp2(ref[SLOTS // 2].astype(jnp.int32).astype(F32) * 0.125) * (1.0 / LIMIT) for ref in parts]
    for o in range(SLOTS // 2):
        total = own[o]
        for ref, scale in zip(parts, scales):
            total = total + ref[o].astype(jnp.int32).astype(F32) * scale[o : o + 1]
        out_ref[o] = total


def finish(own, parts):
    here = pl.BlockSpec(memory_space=pltpu.VMEM)
    return pl.pallas_call(
        finish_kernel,
        in_specs=[here] * 4,
        out_specs=here,
        out_shape=jax.ShapeDtypeStruct(own.shape, F32),
        compiler_params=pltpu.CompilerParams(vmem_limit_bytes=4 * MIB),
        name="finish",
    )(own, *parts)


def along_table(dy, dx):
    return [
        (y * SIDE + x, (y + dy) % SIDE * SIDE + (x + dx) % SIDE) for y in range(SIDE) for x in range(SIDE)
    ]


def along_sector(dz, dc):
    return [(z * 2 + c, (z + dz) % SIDE * 2 + (c ^ dc)) for z in range(SIDE) for c in range(2)]


def local(
    wave_blocks,
    recoupling,
    right_blocks,
    sector_sizes,
    channel_env,
    fetch_list,
    term_pick,
    term_table,
    term_slot,
    term_live,
):
    sector = lax.axis_index("sector")
    place = lax.axis_index("table")
    z, core = sector // 2, sector % 2
    y, x = place // SIDE, place % SIDE

    meta = jnp.concatenate(
        [jnp.stack([core, x, y, z]), channel_env.reshape(-1), sector_sizes, fetch_list.reshape(-1)]
    )

    lines = {0: wave_blocks}
    for d in X_ORDER:
        lines[d] = lax.ppermute(wave_blocks, "table", along_table(0, d))
    lines = [lines[d] for d in range(SIDE)]
    sent = pack(core.reshape(1), recoupling, term_pick, term_table, term_slot, term_live)
    sent, lines = lax.optimization_barrier((sent, lines))
    mine = lax.all_to_all(sent, "table", 0, 0).reshape(TABS * SIDE * SIDE, SENT)
    theirs = lax.ppermute(mine, "sector", along_sector(0, 1))

    planes = {0: jnp.stack(lines)}
    for e in Z_ORDER:
        planes[e] = lax.ppermute(planes[0], "sector", along_sector(e, 0))
    planes = [planes[e] for e in PLANES]
    planes = planes + [lax.ppermute(p, "sector", along_sector(0, 1)) for p in planes]
    own, wave = choose(meta, own_half(mine), planes)
    parts = far_half(meta, mine, theirs, own, wave, right_blocks)
    return finish(parts[0], [lax.ppermute(parts[d], "table", along_table(d, 0)) for d in (2, 1, 3)])


def solution(mesh):
    placed = (
        P("sector", "table", None),
        P("table", None, None),
        P("sector", None, None),
        P("sector"),
        P("sector", None),
        P("sector", None, None),
        P(("sector", "table")),
        P(("sector", "table")),
        P(("sector", "table")),
        P(("sector", "table")),
    )
    return jax.shard_map(
        local, mesh=mesh, in_specs=placed, out_specs=P("sector", "table", None), check_vma=False
    )
```

```python
import functools

import jax
import jax.numpy as jnp
from jax import lax
from jax.experimental import pallas as pl
from jax.experimental.pallas import tpu as pltpu
from jax.sharding import PartitionSpec as P

BF = jnp.bfloat16
F32 = jnp.float32
SIDE = 4
TABS = 16
ROWS = 16
HALF = 64
WIDTH = 256
SLOTS = 16
PICKS = 24
PAIRS = SLOTS * PICKS
SHARE = ROWS * 128
SENT = SHARE + PAIRS
DEPTH = PICKS * HALF
PITCH = PAIRS + 8
ROW_PITCH = ROWS + 8
PACK_MIB = 16
MIB = 1 << 20
ENV = 4
SIZE = ENV + SLOTS
FETCH = SIZE + SLOTS // 2
LISTED = 3
CHUNK = 64
LIMIT = 32700.0
STEP = SLOTS * ROWS
X_ORDER = (2, 1, 3)
Z_ORDER = (2, 1, 3)
PLANES = (0, 2, 1, 3)
CHOOSE_COST = 1_000_000_000
OWN_COST = 100_000_000_000
FAR_COST = 4_000_000_000
WEIGH_COST = 100_000_000_000


def in_hbm(value):
    return pltpu.with_memory_space_constraint(value, pltpu.HBM)


def swap_halves(value):
    return pltpu.roll(value, 64, 1)


def pack_kernel(meta, blocks, pick_in, tab_in, slot_in, live_in, out_ref, held, lists, rows, ready, sems, list_sems, out_sems):
    core = meta[0]

    def fetch(x, u):
        source = blocks.at[:, core + 2 * u, pl.ds(x * ROWS, ROWS), :]
        return pltpu.make_async_copy(source, held.at[x, u], sems.at[x, u])

    def hand(x):
        return pltpu.make_async_copy(ready.at[x], out_ref.at[:, x], out_sems.at[x])

    for x in range(SIDE):
        for u in range(2):
            fetch(x, u).start()
    copies = []
    for n, ref in enumerate((pick_in, tab_in, slot_in, live_in)):
        copies.append(pltpu.make_async_copy(ref, lists.at[n], list_sems.at[n]))
        copies[n].start()
    def count():
        for copy in copies:
            copy.wait()

        terms = pick_in.shape[1]
        tab_hot = (lax.broadcasted_iota(jnp.int32, (TABS, terms), 0) == lists[1]) & (lists[3] > 0)
        pair = lists[2] * PICKS + lists[0]
        pair_hot = lax.broadcasted_iota(jnp.int32, (PAIRS, terms), 0) == pair
        counts = lax.dot_general(
            tab_hot.astype(F32).astype(BF),
            pair_hot.astype(F32).astype(BF),
            (((1,), (1,)), ((), ())),
            preferred_element_type=F32,
        ).astype(BF)
        return counts

    low = lax.broadcasted_iota(jnp.int32, (TABS, 128), 1) < 64
    for x in range(SIDE):
        for u in range(2):
            fetch(x, u).wait()
            for t in range(TABS):
                block = held[x, u, t].astype(F32)
                for k in range(2):
                    rows[k, u, t * ROW_PITCH : t * ROW_PITCH + ROWS, :] = block[:, k * 128 : k * 128 + 128]
        if x == 0:
            counts = count()
        for y in range(SIDE):
            ready[x, y, :, SHARE:SENT] = counts
        for q in range(ROWS):
            lanes = slice(q * 128, q * 128 + 128)
            for k in range(2):
                a = rows[k, 0, pl.ds(q, TABS, stride=ROW_PITCH), :]
                b = rows[k, 1, pl.ds(q, TABS, stride=ROW_PITCH), :]
                mixed = swap_halves(jnp.where(low, b, a))
                ready[x, 2 * k, :, lanes] = jnp.where(low, a, mixed).astype(BF)
                ready[x, 2 * k + 1, :, lanes] = jnp.where(low, mixed, b).astype(BF)
        hand(x).start()
    for x in range(SIDE):
        hand(x).wait()


def pack(meta, recoupling, pick, tab, slot, live):
    there = pl.BlockSpec(memory_space=pltpu.HBM)
    out = pl.pallas_call(
        pack_kernel,
        in_specs=[pl.BlockSpec(memory_space=pltpu.SMEM)] + [there] * 5,
        out_specs=there,
        out_shape=pltpu.HBM((SIDE, SIDE, TABS, SENT), BF),
        scratch_shapes=[
            pltpu.VMEM((SIDE, 2, TABS, ROWS, WIDTH), BF),
            pltpu.VMEM((4, 1, pick.shape[0]), jnp.int32),
            pltpu.VMEM((2, 2, TABS * ROW_PITCH, 128), F32),
            pltpu.VMEM((SIDE, SIDE, TABS, SENT), BF),
            pltpu.SemaphoreType.DMA((SIDE, 2)),
            pltpu.SemaphoreType.DMA((4,)),
            pltpu.SemaphoreType.DMA((SIDE,)),
        ],
        compiler_params=pltpu.CompilerParams(vmem_limit_bytes=PACK_MIB * MIB),
        name="pack",
    )(
        meta,
        in_hbm(recoupling.reshape(TABS, SIDE, HALF, WIDTH)),
        *(in_hbm(v.reshape(1, -1)) for v in (pick, tab, slot, live)),
    )
    return out.reshape(SIDE * SIDE, TABS, SENT)


def weigh(counts_ref, share_ref, sums):
    counts = counts_ref[:, SHARE:SENT]
    for n in range(ROWS // 2):
        part = lax.dot_general(
            counts, share_ref[:, n * 256 : n * 256 + 256], (((0,), (0,)), ((), ())), preferred_element_type=F32
        )
        for k in range(2):
            start = (2 * n + k) * PITCH
            sums[start : start + PAIRS, :] = part[:, k * 128 : k * 128 + 128]


def relay(sums, hi_ref, lo_ref):
    low = lax.broadcasted_iota(jnp.int32, (ROWS, 128), 1) < 64

    for s in range(SLOTS):
        for k in range(PICKS // 2):
            row = s * PICKS + 2 * k
            a = sums[pl.ds(row, ROWS, stride=PITCH), :]
            b = sums[pl.ds(row + 1, ROWS, stride=PITCH), :]
            mixed = swap_halves(jnp.where(low, b, a))
            for u, value in enumerate((jnp.where(low, a, mixed), jnp.where(low, mixed, b))):
                hi = value.astype(BF)
                place = slice((2 * s + u) * ROWS, (2 * s + u + 1) * ROWS)
                hi_ref[place, k * 128 : k * 128 + 128] = hi
                lo_ref[place, k * 128 : k * 128 + 128] = (value - hi.astype(F32)).astype(BF)


def multiply(hi_ref, lo_ref, weights, n):
    rows = slice(n * CHUNK, (n + 1) * CHUNK)
    part = jnp.dot(hi_ref[rows, :], weights, preferred_element_type=F32)
    return part + jnp.dot(lo_ref[rows, :], weights, preferred_element_type=F32)


def own_kernel(mine, sums):
    weigh(mine, mine, sums)


def own_half(mine):
    here = pl.BlockSpec(memory_space=pltpu.VMEM)
    return pl.pallas_call(
        own_kernel,
        in_specs=[here],
        out_specs=here,
        out_shape=pltpu.VMEM((ROWS * PITCH, 128), F32),
        compiler_params=pltpu.CompilerParams(vmem_limit_bytes=16 * MIB),
        cost_estimate=pl.CostEstimate(flops=OWN_COST, bytes_accessed=MIB, transcendentals=0),
        name="own_half",
    )(mine)


def choose_kernel(table, sums, *refs):
    planes, (out_ref, wave, hi_ref, lo_ref, meta, meta_sem) = refs[:8], refs[8:]
    fetch = pltpu.make_async_copy(table, meta, meta_sem)
    fetch.start()
    relay(sums, hi_ref, lo_ref)
    fetch.wait()
    core, x, z = meta[0], meta[1], meta[3]
    for c in range(2):
        for place, e in enumerate(PLANES):
            group = 2 * lax.rem(z - e + SIDE, SIDE) + (core if c == 0 else 1 - core)
            for n in range(LISTED):
                pick = LISTED * group + n
                piece = meta[FETCH + pick]
                for d in range(SIDE):
                    rows = pl.ds(pl.multiple_of(lax.rem(x - d + SIDE, SIDE) * ROWS, ROWS), ROWS)
                    wave[pick, rows, :] = planes[c * SIDE + place][d, piece]
    weights = wave[...].reshape(DEPTH, WIDTH)
    for n in range(2 * STEP // CHUNK):
        out_ref[n * CHUNK : (n + 1) * CHUNK, :] = multiply(hi_ref, lo_ref, weights, n)


def choose(meta, own, planes):
    here = pl.BlockSpec(memory_space=pltpu.VMEM)
    return pl.pallas_call(
        choose_kernel,
        in_specs=[pl.BlockSpec(memory_space=pl.ANY)] + [here] * 9,
        out_specs=[here] * 2,
        out_shape=[pltpu.VMEM((2 * STEP, WIDTH), F32), pltpu.VMEM((PICKS, HALF, WIDTH), BF)],
        scratch_shapes=[
            pltpu.VMEM((2 * STEP, DEPTH), BF),
            pltpu.VMEM((2 * STEP, DEPTH), BF),
            pltpu.SMEM(meta.shape, jnp.int32),
            pltpu.SemaphoreType.DMA(()),
        ],
        compiler_params=pltpu.CompilerParams(vmem_limit_bytes=16 * MIB),
        cost_estimate=pl.CostEstimate(flops=CHOOSE_COST, bytes_accessed=MIB, transcendentals=0),
        name="choose",
    )(meta, own, *planes)


def far_kernel(table, mine, theirs, own, wave, right, s0, s1, s2, s3, sums, hi_ref, lo_ref, channel, codes, meta, meta_sem):
    fetch = pltpu.make_async_copy(table, meta, meta_sem)
    fetch.start()
    codes[...] = jnp.zeros_like(codes)
    weigh(mine, theirs, sums)
    relay(sums, hi_ref, lo_ref)
    fetch.wait()
    core, x, y = meta[0], meta[1], meta[2]
    weights = wave[...].reshape(DEPTH, WIDTH)
    for s in range(SLOTS):
        for u in range(2):
            step = lax.rem(2 * u + core - y + SIDE, SIDE)
            channel[step, s * ROWS : (s + 1) * ROWS, :] = own[(2 * s + u) * ROWS : (2 * s + u + 1) * ROWS, :]
    for n in range(2 * STEP // CHUNK):
        part = multiply(hi_ref, lo_ref, weights, n)
        for m in range(CHUNK // ROWS):
            s, u = divmod(n * (CHUNK // ROWS) + m, 2)
            step = lax.rem(2 * u + 1 - core - y + SIDE, SIDE)
            channel[step, s * ROWS : (s + 1) * ROWS, :] = part[m * ROWS : (m + 1) * ROWS]
    columns = lax.broadcasted_iota(jnp.int32, (ROWS, WIDTH), 1)
    lines = lax.broadcasted_iota(jnp.int32, (ROWS, WIDTH), 0)
    reach = [jnp.maximum(lines + (lax.rem(y + d, SIDE) * SIDE + x) * ROWS, columns) for d in range(SIDE)]
    for o in range(SLOTS // 2):
        hi, lo, env = [], [], []
        for s in (2 * o, 2 * o + 1):
            env.append(right[meta[ENV + s]])
            value = channel[:, s * ROWS : (s + 1) * ROWS, :].reshape(HALF, WIDTH)
            hi.append(value.astype(BF))
            lo.append((value - hi[-1].astype(F32)).astype(BF))
        both = jnp.concatenate([jnp.concatenate(hi, axis=1), jnp.concatenate(lo, axis=1)], axis=0)
        result = jnp.dot(both, jnp.concatenate(env, axis=0), preferred_element_type=F32)
        result = result[:HALF] + result[HALF:]
        size = meta[SIZE + o]
        for d, ref in enumerate((s0, s1, s2, s3)):
            part = jnp.where(reach[d] < size, result[d * ROWS : (d + 1) * ROWS], 0.0)
            if d == 0:
                ref[o] = part
                continue
            peak = jnp.max(jnp.abs(part), axis=0, keepdims=True)
            code = jnp.ceil(jnp.log2(jnp.maximum(peak, 1e-30)) * 8.0 + 0.01)
            scaled = part * (jnp.exp2(code * -0.125) * LIMIT)
            ref[o] = jnp.round(scaled).astype(jnp.int32).astype(jnp.int16)
            codes[d - 1, o : o + 1, :] = code
    for d, ref in enumerate((s1, s2, s3)):
        ref[SLOTS // 2] = codes[d].astype(jnp.int32).astype(jnp.int16)


def far_half(meta, mine, theirs, own, wave, right):
    sectors = SLOTS // 2
    here = pl.BlockSpec(memory_space=pltpu.VMEM)
    return pl.pallas_call(
        far_kernel,
        in_specs=[pl.BlockSpec(memory_space=pl.ANY)] + [here] * 5,
        out_specs=[here] * 4,
        out_shape=[pltpu.VMEM((sectors, ROWS, WIDTH), F32)] + [pltpu.VMEM((sectors + 1, ROWS, WIDTH), jnp.int16)] * 3,
        scratch_shapes=[
            pltpu.VMEM((ROWS * PITCH, 128), F32),
            pltpu.VMEM((2 * STEP, DEPTH), BF),
            pltpu.VMEM((2 * STEP, DEPTH), BF),
            pltpu.VMEM((SIDE, STEP, WIDTH), F32),
            pltpu.VMEM((3, ROWS, WIDTH), F32),
            pltpu.SMEM(meta.shape, jnp.int32),
            pltpu.SemaphoreType.DMA(()),
        ],
        compiler_params=pltpu.CompilerParams(vmem_limit_bytes=24 * MIB),
        cost_estimate=pl.CostEstimate(flops=FAR_COST, bytes_accessed=MIB, transcendentals=0),
        name="far_half",
    )(meta, mine, theirs, own, wave, right)


def finish_kernel(own, *refs):
    parts, out_ref = refs[:-1], refs[-1]
    scales = [jnp.exp2(ref[SLOTS // 2].astype(jnp.int32).astype(F32) * 0.125) * (1.0 / LIMIT) for ref in parts]
    for o in range(SLOTS // 2):
        total = own[o]
        for ref, scale in zip(parts, scales):
            total = total + ref[o].astype(jnp.int32).astype(F32) * scale[o : o + 1]
        out_ref[o] = total


def finish(own, parts):
    here = pl.BlockSpec(memory_space=pltpu.VMEM)
    return pl.pallas_call(
        finish_kernel,
        in_specs=[here] * 4,
        out_specs=here,
        out_shape=jax.ShapeDtypeStruct(own.shape, F32),
        compiler_params=pltpu.CompilerParams(vmem_limit_bytes=4 * MIB),
        name="finish",
    )(own, *parts)


def along_table(dy, dx):
    return [
        (y * SIDE + x, (y + dy) % SIDE * SIDE + (x + dx) % SIDE) for y in range(SIDE) for x in range(SIDE)
    ]


def along_sector(dz, dc):
    return [(z * 2 + c, (z + dz) % SIDE * 2 + (c ^ dc)) for z in range(SIDE) for c in range(2)]


def local(
    wave_blocks,
    recoupling,
    right_blocks,
    sector_sizes,
    channel_env,
    fetch_list,
    term_pick,
    term_table,
    term_slot,
    term_live,
):
    sector = lax.axis_index("sector")
    place = lax.axis_index("table")
    z, core = sector // 2, sector % 2
    y, x = place // SIDE, place % SIDE

    meta = jnp.concatenate(
        [jnp.stack([core, x, y, z]), channel_env.reshape(-1), sector_sizes, fetch_list.reshape(-1)]
    )

    lines = {0: wave_blocks}
    for d in X_ORDER:
        lines[d] = lax.ppermute(wave_blocks, "table", along_table(0, d))
    lines = [lines[d] for d in range(SIDE)]
    sent = pack(core.reshape(1), recoupling, term_pick, term_table, term_slot, term_live)
    sent, lines = lax.optimization_barrier((sent, lines))
    mine = lax.all_to_all(sent, "table", 0, 0).reshape(TABS * SIDE * SIDE, SENT)
    theirs = lax.ppermute(mine, "sector", along_sector(0, 1))

    planes = {0: jnp.stack(lines)}
    for e in Z_ORDER:
        planes[e] = lax.ppermute(planes[0], "sector", along_sector(e, 0))
    planes = [planes[e] for e in PLANES]
    planes = planes + [lax.ppermute(p, "sector", along_sector(0, 1)) for p in planes]
    own, wave = choose(meta, own_half(mine), planes)
    parts = far_half(meta, mine, theirs, own, wave, right_blocks)
    return finish(parts[0], [lax.ppermute(parts[d], "table", along_table(d, 0)) for d in (2, 1, 3)])


def solution(mesh):
    placed = (
        P("sector", "table", None),
        P("table", None, None),
        P("sector", None, None),
        P("sector"),
        P("sector", None),
        P("sector", None, None),
        P(("sector", "table")),
        P(("sector", "table")),
        P(("sector", "table")),
        P(("sector", "table")),
    )
    return jax.shard_map(
        local, mesh=mesh, in_specs=placed, out_specs=P("sector", "table", None), check_vma=False
    )
```
